128 devices in a mesh: dp: 32 (over z, y_hi, x), row: 2 (over core), col: 2 (over y_lo).
Axes of the slice: x: 4, y: 4 (y_hi: 2, y_lo: 2; y = y_hi * 2 + y_lo), z: 4, core: 2. Of those that a mesh axis runs over, the one named last changes fastest.
Arguments:
- hidden_in: bfloat16 [32768, 1536], P(('dp', 'row'), 'col'), may hold values from -64 to 64
- gain_attn: float32 [1536], P('col'), may hold values from 0.25 to 3.5
- w_query: bfloat16 [1536, 1536], P('col', 'row'), may hold values from -0.21875 to 0.21875
- w_key: bfloat16 [1536, 768], P('col', 'row'), may hold values from -0.21875 to 0.21875
- w_value: bfloat16 [1536, 768], P('col', 'row'), may hold values from -0.15625 to 0.15625
- w_out: bfloat16 [1536, 1536], P('row', 'col'), may hold values from -0.4375 to 0.4375
- gain_mlp: float32 [1536], P('col'), may hold values from 0.25 to 3.5
- w_gate: bfloat16 [1536, 4096], P('col', 'row'), may hold values from -0.15625 to 0.15625
- w_up: bfloat16 [1536, 4096], P('col', 'row'), may hold values from -0.15625 to 0.15625
- w_down: bfloat16 [4096, 1536], P('row', 'col'), may hold values from -0.1875 to 0.1875
- out_grad: bfloat16 [32768, 1536], P(('dp', 'row'), 'col'), may hold values from -42 to 42
Outputs:
- block_out: bfloat16 [32768, 1536], P(('dp', 'row'), 'col')
- in_grad: bfloat16 [32768, 1536], P(('dp', 'row'), 'col')
- grad_gain_attn: float32 [1536], P('col')
- grad_w_query: float32 [1536, 1536], P('col', 'row')
- grad_w_key: float32 [1536, 768], P('col', 'row')
- grad_w_value: float32 [1536, 768], P('col', 'row')
- grad_w_out: float32 [1536, 1536], P('row', 'col')
- grad_gain_mlp: float32 [1536], P('col')
- grad_w_gate: float32 [1536, 4096], P('col', 'row')
- grad_w_up: float32 [1536, 4096], P('col', 'row')
- grad_w_down: float32 [4096, 1536], P('row', 'col')
The draws below stay inside these ranges and needn't reach their ends.
All inputs are finite; a program needn't handle non-finite values.
Results may differ from the reference program's by a relative error of at most 0.03.
Values may be sent and summed in bfloat16 or wider, within the bound.
A program may use at most 256 MiB of HBM per device.

```python
import math
import jax
import jax.numpy as jnp
from jax import lax

D = 1536
HEADS = 16
KV_HEADS = 8
HEAD_DIM = 96
FF = 4096
LEN = 1024
KVD = 768
TOKENS = 32768
N_DP = 32


def rising_gain(key, ratio):
    rise = jnp.exp(math.log(ratio) * (jnp.arange(D, dtype=jnp.float32) / (D - 1) - 0.5))
    jitter = jax.random.uniform(key, (D,), minval=0.85, maxval=1.15)
    return rise * jitter


def draw_gain_attn(key, part):
    key = jax.random.fold_in(key, 21)
    return rising_gain(key, 4.0).astype(jnp.float32)


def draw_gain_mlp(key, part):
    key = jax.random.fold_in(key, 33)
    return rising_gain(key, 4.0).astype(jnp.float32)


def draw_hidden_in(key, part):
    key = jax.random.fold_in(key, 5)
    base_key, row_key, col_key = jax.random.split(key, 3)
    spread = jnp.exp(jax.random.uniform(col_key, (D,), minval=math.log(0.3), maxval=math.log(3.0)))
    rise = jnp.exp(math.log(3.0) * (jnp.arange(D, dtype=jnp.float32) / (D - 1) - 0.5))
    base = jax.random.truncated_normal(base_key, -4.0, 4.0, (TOKENS, D))
    scales = jnp.exp(jax.random.uniform(row_key, (TOKENS,), minval=math.log(0.3), maxval=math.log(3.0)))
    return (base * scales[:, None] * (spread * rise)[None, :]).astype(jnp.bfloat16)


def draw_out_grad(key, part):
    key = jax.random.fold_in(key, 9)
    base_key, row_key, col_key = jax.random.split(key, 3)
    rise = jnp.exp(math.log(3.0) * (jnp.arange(TOKENS, dtype=jnp.float32) / (TOKENS - 1) - 0.5))
    scales = jnp.exp(jax.random.uniform(row_key, (TOKENS,), minval=math.log(0.3), maxval=math.log(3.0)))
    spread = jnp.exp(jax.random.uniform(col_key, (D,), minval=math.log(0.5), maxval=math.log(2.0)))
    base = jax.random.truncated_normal(base_key, -4.0, 4.0, (TOKENS, D))
    return (base * (rise * scales)[:, None] * spread[None, :]).astype(jnp.bfloat16)


def levels(stream_key, shape, cuts, low, top_value):
    level = 1.0
    for dim, blocks in cuts:
        steps = jax.random.uniform(jax.random.fold_in(jax.random.fold_in(stream_key, 6), dim), (blocks,), jnp.float32, low / len(cuts), top_value / len(cuts))
        level = level * jnp.repeat(jnp.exp(steps), shape[dim] // blocks).reshape((-1,) + (1,) * (len(shape) - 1 - dim))
    return level


def bell_draw(own_key, shape, width, reach, cuts=(), held_as=jnp.bfloat16):
    values = jax.random.normal(own_key, shape, jnp.float32) * width
    if len(cuts) > 0:
        values = levels(own_key, shape, cuts, -0.22, 0.18) * values
    return jnp.clip(values, min=-reach, max=reach).astype(held_as)


def setup_inputs(seed: int = 0) -> dict:
    arg_keys = jax.random.split(jax.random.key(seed), 12)
    hidden_in = draw_hidden_in(jax.random.fold_in(arg_keys[11], 71), 0)
    gain_attn = draw_gain_attn(jax.random.fold_in(arg_keys[11], 71), 0)
    w_query = bell_draw(arg_keys[2], (D, D), (D // 2) ** -0.5, 0.21875, ((0, 2), (1, 2)))
    w_key = bell_draw(arg_keys[3], (D, KVD), (D // 2) ** -0.5, 0.21875, ((0, 2), (1, 2)))
    w_value = bell_draw(arg_keys[4], (D, KVD), D ** -0.5, 0.15625, ((0, 2), (1, 2)))
    w_out = bell_draw(arg_keys[5], (D, D), (D // 8) ** -0.5, 0.4375, ((0, 2), (1, 2)))
    gain_mlp = draw_gain_mlp(jax.random.fold_in(arg_keys[11], 71), 0)
    w_gate = bell_draw(arg_keys[7], (D, FF), D ** -0.5, 0.15625, ((0, 2), (1, 2)))
    w_up = bell_draw(arg_keys[8], (D, FF), D ** -0.5, 0.15625, ((0, 2), (1, 2)))
    w_down = bell_draw(arg_keys[9], (FF, D), (FF // 4) ** -0.5, 0.1875, ((0, 2), (1, 2)))
    out_grad = draw_out_grad(jax.random.fold_in(arg_keys[11], 71), 0)
    return {"hidden_in": hidden_in, "gain_attn": gain_attn, "w_query": w_query, "w_key": w_key, "w_value": w_value, "w_out": w_out, "gain_mlp": gain_mlp, "w_gate": w_gate, "w_up": w_up, "w_down": w_down, "out_grad": out_grad}


@jax.custom_vjp
def low(v):
    return lax.optimization_barrier(v.astype(jnp.bfloat16)).astype(jnp.float32)

@jax.custom_vjp
def low_back(v):
    return v

def low_keep(v):
    return (low(v), None)

def low_pass(kept, grad):
    return (grad,)

def back_keep(v):
    return (v, None)

def back_low(kept, grad):
    return (low(grad),)
low.defvjp(low_keep, low_pass)
low_back.defvjp(back_keep, back_low)
EPS = 1e-05
ROPE_BASE = 100000.0
NEG = -1e+30
HIGH = lax.Precision.HIGHEST

def matmul(left, right):
    return jnp.dot(left, right, precision=HIGH, preferred_element_type=jnp.float32)

def rms_scale(value, gain):
    return value * lax.rsqrt(lax.optimization_barrier(jnp.mean(value * value, axis=-1, keepdims=True)) + EPS) * gain

def rotate(value, cosine, sine):
    half = value.shape[-1] // 2
    first = value[..., :half]
    second = value[..., half:]
    return jnp.concatenate([first * cosine - second * sine, second * cosine + first * sine], axis=-1)

def attend_sequence(item):
    query, keys, values = item
    group = HEADS // KV_HEADS
    keys_wide = jnp.repeat(keys, group, axis=1)
    values_wide = jnp.repeat(values, group, axis=1)
    block = min(512, LEN)
    scale = 1.0 / math.sqrt(HEAD_DIM)
    pieces = query.reshape(LEN // block, block, HEADS, HEAD_DIM)
    starts = (jnp.arange(LEN // block) * block).astype(jnp.int32)

    def one_block(entry):
        piece, start = entry
        raw = low_back(jnp.einsum('qhd,khd->hqk', piece, keys_wide, precision=HIGH))
        places = start + jnp.arange(block).astype(jnp.int32)
        causal = jnp.arange(LEN).astype(jnp.int32)[None, None, :] <= places[None, :, None]
        scores = jnp.where(causal, raw * scale, NEG)
        top = lax.optimization_barrier(jnp.max(scores, axis=-1, keepdims=True))
        powers = jnp.exp(scores - top)
        shares = low(powers / lax.optimization_barrier(jnp.sum(powers, axis=-1, keepdims=True)))
        return jnp.einsum('hqk,khd->qhd', shares, values_wide, precision=HIGH)
    return lax.map(jax.checkpoint(one_block), (pieces, starts)).reshape(LEN, HEADS, HEAD_DIM)

def layer(resid, gain_attn, w_query, w_key, w_value, w_out, gain_mlp, w_gate, w_up, w_down):
    count = resid.shape[0]
    half = HEAD_DIM // 2
    rates = jnp.exp(-math.log(ROPE_BASE) * 2.0 * jnp.arange(half).astype(jnp.float32) / HEAD_DIM)
    places = (jnp.arange(count) % LEN).astype(jnp.float32)
    angle = places[:, None] * rates[None, :]
    cosine = jnp.cos(angle)[:, None, :]
    sine = jnp.sin(angle)[:, None, :]
    scaled_attn = low(rms_scale(resid, gain_attn))
    query_pre = low_back(matmul(scaled_attn, w_query)).reshape(count, HEADS, HEAD_DIM)
    key_pre = low_back(matmul(scaled_attn, w_key)).reshape(count, KV_HEADS, HEAD_DIM)
    value_pre = low_back(matmul(scaled_attn, w_value)).reshape(count, KV_HEADS, HEAD_DIM)
    query = low(rotate(query_pre, cosine, sine)).reshape(count // LEN, LEN, HEADS, HEAD_DIM)
    keys = low(rotate(key_pre, cosine, sine)).reshape(count // LEN, LEN, KV_HEADS, HEAD_DIM)
    values = low(value_pre).reshape(count // LEN, LEN, KV_HEADS, HEAD_DIM)
    attended = lax.map(attend_sequence, (query, keys, values))
    attended = low(low_back(attended.reshape(count, D)))
    middle = resid + low_back(matmul(attended, w_out))
    scaled_mlp = low(rms_scale(middle, gain_mlp))
    gate = low_back(matmul(scaled_mlp, w_gate))
    upper = low_back(matmul(scaled_mlp, w_up))
    hidden = low(jax.nn.silu(gate) * upper)
    return middle + matmul(hidden, w_down)

def reference(hidden_in, gain_attn, w_query, w_key, w_value, w_out, gain_mlp, w_gate, w_up, w_down, out_grad):
    params = tuple((item.astype(jnp.float32) for item in (gain_attn, w_query, w_key, w_value, w_out, gain_mlp, w_gate, w_up, w_down)))
    limit = min(max(1, 4096 // LEN), N_DP)
    group_seqs = max((k for k in range(1, limit + 1) if N_DP % k == 0))
    count = group_seqs * LEN
    blocks = TOKENS // count
    inputs = hidden_in.astype(jnp.float32).reshape(blocks, count, D)
    cotangents = out_grad.astype(jnp.float32).reshape(blocks, count, D)

    def step(totals, item):
        block_in, block_grad = item

        def apply(resid, *weights):
            return layer(resid, *weights)
        result, pull = jax.vjp(apply, block_in, *params)
        grads = pull(block_grad)
        totals = tuple((total + grad for total, grad in zip(totals, grads[1:])))
        return (totals, (result.astype(jnp.bfloat16), grads[0].astype(jnp.bfloat16)))
    zeros = tuple((jnp.zeros_like(item) for item in params))
    totals, (outputs, in_grads) = lax.scan(step, zeros, (inputs, cotangents))
    return (outputs.reshape(TOKENS, D), in_grads.reshape(TOKENS, D), totals[0], totals[1], totals[2], totals[3], totals[4], totals[5], totals[6], totals[7], totals[8])
```

```python
import functools
import math

import jax
import jax.numpy as jnp
from jax import lax
from jax.experimental import pallas as pl
from jax.experimental.pallas import tpu as pltpu
from jax.sharding import PartitionSpec as P

MESH = pl.DeviceIdType.MESH
BF16 = jnp.bfloat16
F32 = jnp.float32
TYPES = 6
LANE_DIMS = ("xa", "xb", "za", "zb")
ALL_DIMS = ("xa", "xb", "ya", "yb", "za", "zb")


class Place:
    def __init__(self):
        dp = lax.axis_index("dp")
        self.row = lax.axis_index("row")
        self.col = lax.axis_index("col")
        self.x = dp % 4
        self.yh = (dp // 4) % 2
        self.z = dp // 8
        y = self.yh * 2 + self.col
        self.bit = {
            "xa": ((self.x + 1) // 2) % 2,
            "xb": self.x // 2,
            "ya": ((y + 1) // 2) % 2,
            "yb": y // 2,
            "za": ((self.z + 1) // 2) % 2,
            "zb": self.z // 2,
        }

    def partner(self, dim):
        x, yh, z, row, col = self.x, self.yh, self.z, self.row, self.col
        if dim == "xa":
            x = x + 1 - 2 * (x % 2)
        elif dim == "xb":
            x = 3 - x
        elif dim == "za":
            z = z + 1 - 2 * (z % 2)
        elif dim == "zb":
            z = 3 - z
        elif dim in ("ya", "col"):
            col = 1 - col
        elif dim == "yb":
            col = 1 - col
            yh = 1 - yh
        elif dim == "y2":
            yh = 1 - yh
        elif dim == "row":
            row = 1 - row
        return ((z * 2 + yh) * 4 + x, row, col)


def greet(place, dims):
    barrier = pltpu.get_barrier_semaphore()
    for dim in dims:
        pl.semaphore_signal(barrier, inc=1, device_id=place.partner(dim), device_id_type=MESH)
    pl.semaphore_wait(barrier, len(dims))


def remote(place, dim, src, dst, send_sem, recv_sem):
    return pltpu.make_async_remote_copy(
        src_ref=src,
        dst_ref=dst,
        send_sem=send_sem,
        recv_sem=recv_sem,
        device_id=place.partner(dim),
        device_id_type=MESH,
    )


def exchange(value, dim, ident):
    def kernel(src, dst, send_sem, recv_sem):
        place = Place()
        greet(place, (dim,))
        copy = remote(place, dim, src, dst, send_sem, recv_sem)
        copy.start()
        copy.wait()

    return pl.pallas_call(
        kernel,
        out_shape=jax.ShapeDtypeStruct(value.shape, value.dtype),
        in_specs=[pl.BlockSpec(memory_space=pl.ANY)],
        out_specs=pl.BlockSpec(memory_space=pl.ANY),
        scratch_shapes=[pltpu.SemaphoreType.DMA, pltpu.SemaphoreType.DMA],
        compiler_params=pltpu.CompilerParams(collective_id=ident, has_side_effects=True),
        name="exchange_" + dim,
    )(value)


def span(kind, width, fixed):
    if kind == "tall":
        start, size = 0, width
        for bit in fixed:
            size //= 2
            start = start + bit * size
        return pl.ds(pl.multiple_of(start, 16) if fixed else 0, size), pl.ds(0, 128)
    rows, cols, row_start, col_start = 128, width, 0, 0
    for index, bit in enumerate(fixed):
        if index < 3:
            rows //= 2
            row_start = row_start + bit * rows
        else:
            cols //= 2
            col_start = col_start + bit * cols
    if len(fixed) > 0:
        row_start = pl.multiple_of(row_start, 16)
    if len(fixed) > 3:
        col_start = pl.multiple_of(col_start, 128)
    return pl.ds(row_start, rows), pl.ds(col_start, cols)


GATHER_ORDERS = (
    ("xa", "xb", "za", "zb"),
    ("xb", "xa", "zb", "za"),
    ("za", "zb", "xa", "xb"),
    ("zb", "za", "xb", "xa"),
)


class WeightGather:
    def __init__(self, place, kind, width, source, target, send_sem, recv_sem):
        self.place, self.kind, self.width = place, kind, width
        self.source, self.target = source, target
        self.send_sem, self.recv_sem = send_sem, recv_sem

    def part(self, ref, chunk, fixed, half=None):
        rows, cols = span(self.kind, self.width, fixed)
        base = 0 if half is None else half * 768
        if self.kind == "tall":
            return ref.at[rows, pl.ds(pl.multiple_of(base + chunk * 128, 128), 128)]
        return ref.at[pl.ds(pl.multiple_of(base + chunk * 128 + rows.start, 16), rows.size), cols]

    def copy(self, chunk, step):
        place = self.place
        me, other = place.col, 1 - place.col
        sems = (self.send_sem.at[chunk, step], self.recv_sem.at[chunk, step])
        if chunk >= 4:
            dim = "ya" if chunk == 4 else "yb"
            return remote(place, dim, self.part(self.source, chunk, ()), self.part(self.target, chunk, (), me), *sems)
        order = GATHER_ORDERS[chunk]
        bits = [place.bit[dim] for dim in reversed(order)]
        if step == 0:
            dim = "ya" if chunk < 2 else "yb"
            return remote(place, dim, self.part(self.source, chunk, bits), self.part(self.target, chunk, bits, me), *sems)
        bits = bits[: 5 - step]
        part = self.part(self.target, chunk, bits, other)
        return remote(place, order[step - 1], part, part, *sems)

    def begin(self, chunks):
        for chunk in chunks:
            self.copy(chunk, 0).start()

    def advance(self, step):
        for chunk in range(4):
            self.copy(chunk, step - 1).wait_recv()
            self.copy(chunk, step).start()

    def finish(self):
        for chunk in range(TYPES):
            self.copy(chunk, 4 if chunk < 4 else 0).wait_recv()

    def drain(self):
        for chunk in range(TYPES):
            for step in range(5 if chunk < 4 else 1):
                self.copy(chunk, step).wait_send()


def gather_weights(w_att, w_gate, w_up, w_down, tokens, gains, ident):
    kinds = (("wide", 2304), ("wide", 2048), ("wide", 2048), ("tall", 2048))

    def kernel(att, gate, up, down, tok, gain, att_out, gate_out, up_out, down_out, tok_out, gain_out,
               att_held, gate_held, up_held, down_held, send_sem, recv_sem, local_sem, small_send, small_recv):
        place = Place()
        greet(place, ALL_DIMS)
        sources = (att, gate, up, down)
        targets = (att_out, gate_out, up_out, down_out)
        held = (att_held, gate_held, up_held, down_held)
        small = [
            remote(place, "ya", tok.at[:, 1 - place.col], tok_out, small_send.at[0], small_recv.at[0]),
            remote(place, "ya", gain, gain_out, small_send.at[1], small_recv.at[1]),
        ]
        for copy in small:
            copy.start()
        jobs = [
            WeightGather(place, kind, width, source, target, send_sem.at[index], recv_sem.at[index])
            for index, ((kind, width), source, target) in enumerate(zip(kinds, sources, targets))
        ]
        for job in jobs:
            job.begin(range(4))
        for job in jobs:
            job.begin(range(4, 6))
        loads = [
            pltpu.make_async_copy(source, here, local_sem.at[0, index])
            for index, (source, here) in enumerate(zip(sources, held))
        ]
        half = pl.ds(pl.multiple_of(place.col * 768, 128), 768)
        stores = [
            pltpu.make_async_copy(
                here, target.at[:, half] if kind == "tall" else target.at[half], local_sem.at[1, index]
            )
            for index, ((kind, _), here, target) in enumerate(zip(kinds, held, targets))
        ]
        for copy in loads:
            copy.start()
        for load, store in zip(loads, stores):
            load.wait()
            store.start()
        for step in range(1, 5):
            for job in jobs:
                job.advance(step)
        for job in jobs:
            job.finish()
        for copy in stores:
            copy.wait()
        for copy in small:
            copy.wait()
        for job in jobs:
            job.drain()

    anywhere = pl.BlockSpec(memory_space=pl.ANY)
    return pl.pallas_call(
        kernel,
        out_shape=[
            jax.ShapeDtypeStruct((1536, 2304), BF16),
            jax.ShapeDtypeStruct((1536, 2048), BF16),
            jax.ShapeDtypeStruct((1536, 2048), BF16),
            jax.ShapeDtypeStruct((2048, 1536), BF16),
            jax.ShapeDtypeStruct((2, 256, 768), BF16),
            jax.ShapeDtypeStruct(gains.shape, F32),
        ],
        in_specs=[anywhere] * 6,
        out_specs=[anywhere] * 6,
        scratch_shapes=[
            pltpu.VMEM((768, 2304), BF16),
            pltpu.VMEM((768, 2048), BF16),
            pltpu.VMEM((768, 2048), BF16),
            pltpu.VMEM((2048, 768), BF16),
            pltpu.SemaphoreType.DMA((4, TYPES, 5)),
            pltpu.SemaphoreType.DMA((4, TYPES, 5)),
            pltpu.SemaphoreType.DMA((2, 4)),
            pltpu.SemaphoreType.DMA((2,)),
            pltpu.SemaphoreType.DMA((2,)),
        ],
        compiler_params=pltpu.CompilerParams(
            collective_id=ident, has_side_effects=True, vmem_limit_bytes=32 << 20
        ),
        name="gather_weights",
    )(w_att, w_gate, w_up, w_down, tokens, gains)


SUM_ORDERS = (
    ("xa", "xb", "ya", "yb", "za", "zb"),
    ("xb", "xa", "yb", "ya", "zb", "za"),
    ("ya", "yb", "za", "zb", "xa", "xb"),
    ("yb", "ya", "zb", "za", "xb", "xa"),
    ("za", "zb", "xa", "xb", "ya", "yb"),
    ("zb", "za", "xb", "xa", "yb", "ya"),
)
ALL_HALVES = pl.ds(0, 2)


class GradSum:
    def __init__(self, place, kind, width, first, held, landing, out, sems):
        self.place, self.kind, self.width = place, kind, width
        self.first, self.held, self.landing, self.out = first, held, landing, out
        self.send_sem, self.recv_sem, self.ag_send, self.ag_recv, self.own_sem = sems

    def view(self, ref, half, chunk, fixed):
        rows, cols = span(self.kind, self.width, fixed)
        return ref.at[half, chunk, rows, cols]

    def moves(self, chunk, step):
        place = self.place
        order = SUM_ORDERS[chunk]
        dim = order[step]
        regular = [d for d in order if d != "ya"]
        p, q, c = place.bit["ya"], place.bit["yb"], place.col
        y_at = [i for i, d in enumerate(order) if d[0] == "y"]
        a_first = order[y_at[0]] == "ya"
        own = [place.bit[d] for d in order[:step] if d != "ya"]
        flipped = [1 - bit for bit in own]
        if dim[0] != "y":
            bit = place.bit[dim]
            if step < y_at[0]:
                half_own = half_land = ALL_HALVES
            else:
                half_own = c
                half_land = c if a_first else 1 - c
            sent = [(half_own, own + [1 - bit])]
            lands = [(half_land, flipped + [1 - bit])]
            kept = [(half_own, own + [bit])]
            landed = [(half_land, flipped + [bit])]
            return dim, sent, lands, kept, landed
        if a_first and dim == "ya":
            sent = [(1 - p, own + [0]), (p, own + [1])]
            lands = [(1 - p, flipped + [0]), (p, flipped + [1])]
            kept = [(p, own + [0]), (1 - p, own + [1])]
            landed = [(p, flipped + [0]), (1 - p, flipped + [1])]
        elif a_first:
            send_half = (p + 1 - q) % 2
            sent = [(send_half, own + [1 - q])]
            lands = [(c, flipped + [1 - q])]
            kept = [(c, own + [q])]
            landed = [(1 - c, flipped + [q])]
        elif dim == "yb":
            sent = [(ALL_HALVES, own + [1 - q])]
            lands = [(ALL_HALVES, flipped + [1 - q])]
            kept = [(ALL_HALVES, own + [q])]
            landed = [(ALL_HALVES, flipped + [q])]
        else:
            sent = [(1 - c, own)]
            lands = [(1 - c, flipped)]
            kept = [(c, own)]
            landed = [(c, flipped)]
        return dim, sent, lands, kept, landed

    def sends(self, chunk, step):
        dim, sent, lands, _, _ = self.moves(chunk, step)
        source = self.first if step == 0 else self.held
        return [
            remote(
                self.place,
                dim,
                self.view(source, *region),
                self.view(self.landing, *there),
                self.send_sem.at[chunk, step, index],
                self.recv_sem.at[chunk, step, index],
            )
            for index, (region, there) in enumerate(zip(
                [(h, chunk, b) for h, b in sent], [(h, chunk, b) for h, b in lands]
            ))
        ]

    def start(self, step):
        for chunk in range(TYPES):
            for copy in self.sends(chunk, step):
                copy.start()

    def add(self, step):
        for chunk in range(TYPES):
            for copy in self.sends(chunk, step):
                copy.wait_recv()
            _, _, _, kept, landed = self.moves(chunk, step)
            for (half, bits), (from_half, from_bits) in zip(kept, landed):
                rows, cols = span(self.kind, self.width, bits)
                from_rows, from_cols = span(self.kind, self.width, from_bits)
                halves = 2 if half is ALL_HALVES else 1
                block = 16
                for h in range(halves):
                    here = h if halves == 2 else half
                    there = h if halves == 2 else from_half

                    def body(i, carry, here=here, there=there, rows=rows, cols=cols, from_rows=from_rows, from_cols=from_cols, chunk=chunk):
                        mine = (here, chunk, pl.ds(pl.multiple_of(rows.start + i * block, 16), block), cols)
                        came = (there, chunk, pl.ds(pl.multiple_of(from_rows.start + i * block, 16), block), from_cols)
                        self.held[mine] = self.held[mine] + self.landing[came]
                        return carry

                    lax.fori_loop(0, rows.size // block, body, 0)
            if step < 5:
                for copy in self.sends(chunk, step + 1):
                    copy.start()


    def spread(self, chunk, step):
        place = self.place
        order = SUM_ORDERS[chunk]
        stages = []
        for d in reversed(order):
            if d[0] == "y":
                if "y2" not in stages:
                    stages.append("y2")
            else:
                stages.append(d)
        dim = stages[step]
        keep = [d for d in order if d != "ya"]
        done = set(stages[:step])
        bits = [place.bit[d] for d in keep if ("y2" if d == "yb" else d) not in done]
        rows, cols = span(self.kind, self.width, bits)
        target = self.out.at[chunk, rows, cols]
        source = self.held.at[place.col, chunk, rows, cols] if step == 0 else target
        return remote(place, dim, source, target, self.ag_send.at[chunk, step], self.ag_recv.at[chunk, step])

    def own(self, chunk):
        place = self.place
        bits = [place.bit[d] for d in SUM_ORDERS[chunk] if d != "ya"]
        rows, cols = span(self.kind, self.width, bits)
        return pltpu.make_async_copy(
            self.held.at[place.col, chunk, rows, cols], self.out.at[chunk, rows, cols], self.own_sem.at[chunk]
        )

    def spread_start(self):
        for chunk in range(TYPES):
            self.spread(chunk, 0).start()
            self.own(chunk).start()

    def spread_next(self, step):
        for chunk in range(TYPES):
            if step == 1:
                self.own(chunk).wait()
            self.spread(chunk, step - 1).wait_recv()
            self.spread(chunk, step).start()

    def finish(self):
        for chunk in range(TYPES):
            self.spread(chunk, 4).wait_recv()

    def drain(self):
        for chunk in range(TYPES):
            for step in range(6):
                for copy in self.sends(chunk, step):
                    copy.wait_send()
            for step in range(5):
                self.spread(chunk, step).wait_send()


GROUPS = (("tall", 2048), ("wide", 2048), ("wide", 2048), ("wide", 2560))


def group_shape(kind, width):
    return (2048, 128) if kind == "tall" else (128, width)


def sum_gradients(parts, ident):
    count = len(GROUPS)

    def kernel(*refs):
        given, outs = refs[:count], refs[count : 2 * count]
        held, landing = refs[2 * count : 3 * count], refs[3 * count : 4 * count]
        send_sem, recv_sem, ag_send, ag_recv, own_sem, local_sem = refs[4 * count :]
        place = Place()
        greet(place, ALL_DIMS + ("y2",))
        jobs = [
            GradSum(
                place, kind, width, given[g], held[g], landing[g], outs[g],
                (send_sem.at[g], recv_sem.at[g], ag_send.at[g], ag_recv.at[g], own_sem.at[g]),
            )
            for g, (kind, width) in enumerate(GROUPS)
        ]
        loads = [pltpu.make_async_copy(given[g], held[g], local_sem.at[g]) for g in range(count)]
        for g in range(count):
            loads[g].start()
        jobs[0].start(0)
        jobs[1].start(0)
        steps = 6 + 6
        for wave in range(count + steps):
            if wave + 2 < count:
                jobs[wave + 2].start(0)
            for g in range(count):
                step = wave - g
                if step == 0:
                    loads[g].wait()
                if 0 <= step < 6:
                    jobs[g].add(step)
            for g in range(count):
                step = wave - g
                if step == 5:
                    jobs[g].spread_start()
                if 6 <= step < 10:
                    jobs[g].spread_next(step - 5)
                if step == 10:
                    jobs[g].finish()
        for job in jobs:
            job.drain()

    anywhere = pl.BlockSpec(memory_space=pl.ANY)
    shapes = [group_shape(*group) for group in GROUPS]
    return pl.pallas_call(
        kernel,
        out_shape=[jax.ShapeDtypeStruct((TYPES,) + shape, BF16) for shape in shapes],
        in_specs=[anywhere] * count,
        out_specs=[anywhere] * count,
        scratch_shapes=[pltpu.VMEM((2, TYPES) + shape, BF16) for shape in shapes] * 2
        + [
            pltpu.SemaphoreType.DMA((count, TYPES, 6, 2)),
            pltpu.SemaphoreType.DMA((count, TYPES, 6, 2)),
            pltpu.SemaphoreType.DMA((count, TYPES, 5)),
            pltpu.SemaphoreType.DMA((count, TYPES, 5)),
            pltpu.SemaphoreType.DMA((count, TYPES)),
            pltpu.SemaphoreType.DMA((count,)),
        ],
        compiler_params=pltpu.CompilerParams(
            collective_id=ident, has_side_effects=True, vmem_limit_bytes=60 << 20
        ),
        name="sum_gradients",
    )(*parts)


HEAD_DIM = 96
EPS = 1e-05
ROPE_BASE = 100000.0
NEG = -1e30


def matmul(left, right):
    return jnp.dot(left, right, preferred_element_type=F32)


def inner_left(left, right):
    return lax.dot_general(left, right, (((0,), (0,)), ((), ())), preferred_element_type=F32)


def inner_right(left, right):
    return lax.dot_general(left, right, (((1,), (1,)), ((), ())), preferred_element_type=F32)


def ordered(index, own, other, axis):
    return jnp.where(
        index == 0, jnp.concatenate([own, other], axis=axis), jnp.concatenate([other, own], axis=axis)
    )


def rotary(places):
    half = HEAD_DIM // 2
    rates = jnp.exp(-math.log(ROPE_BASE) * 2.0 * jnp.arange(half, dtype=F32) / HEAD_DIM)
    angle = places.astype(F32)[:, None] * rates[None, :]
    return (jnp.cos(angle)[:, None, :], jnp.sin(angle)[:, None, :])


def rotate(value, cosine, sine):
    half = value.shape[-1] // 2
    first, second = value[..., :half], value[..., half:]
    return jnp.concatenate([first * cosine - second * sine, second * cosine + first * sine], axis=-1)


def norm_forward(resid, gain):
    factor = lax.rsqrt(jnp.mean(resid * resid, axis=1, keepdims=True) + EPS)
    normed = resid * factor
    return normed, factor, (normed * gain).astype(BF16)


def norm_backward(grad_scaled, normed, factor, gain):
    grad_normed = grad_scaled * gain
    projection = jnp.mean(grad_normed * normed, axis=1, keepdims=True)
    return factor * (grad_normed - normed * projection), jnp.sum(grad_scaled * normed, axis=0)


def row_gather(value, row, ident):
    return ordered(row, value, exchange(value, "row", ident), 0)


def row_sum(value, row, ident):
    mine = lax.dynamic_slice_in_dim(value, row * 256, 256, 0)
    theirs = lax.dynamic_slice_in_dim(value, (1 - row) * 256, 256, 0)
    return mine + exchange(theirs, "row", ident)


SCALE = 1.0 / math.sqrt(HEAD_DIM)


def attention_blocks(col):
    return ((0, 512, col * 256), (256, 1024, 512 + col * 256))


def scores_of(piece, keys, start):
    raw = jnp.einsum("qkgd,tkd->kgqt", piece, keys, preferred_element_type=F32)
    reach = keys.shape[0]
    causal = jnp.arange(reach)[None, :] <= (start + jnp.arange(256))[:, None]
    return jnp.where(causal, raw * SCALE, NEG)


def attend(query, keys, values, col):
    outputs, logs = [], []
    for at, reach, start in attention_blocks(col):
        piece = query[at : at + 256].reshape(256, 4, 2, HEAD_DIM)
        scores = scores_of(piece, keys[:reach], start)
        top = jnp.max(scores, axis=-1, keepdims=True)
        powers = jnp.exp(scores - top)
        total = jnp.sum(powers, axis=-1, keepdims=True)
        shares = (powers / total).astype(BF16)
        mixed = jnp.einsum("kgqt,tkd->qkgd", shares, values[:reach], preferred_element_type=F32)
        outputs.append(mixed.reshape(256, 8 * HEAD_DIM))
        logs.append(top + jnp.log(total))
    return jnp.concatenate(outputs, axis=0), logs


def attend_back(query, keys, values, grad_out, logs, col):
    grad_queries = []
    grad_keys = jnp.zeros(keys.shape, F32)
    grad_values = jnp.zeros(values.shape, F32)
    for (at, reach, start), log in zip(attention_blocks(col), logs):
        piece = query[at : at + 256].reshape(256, 4, 2, HEAD_DIM)
        back = grad_out[at : at + 256].reshape(256, 4, 2, HEAD_DIM)
        shares = jnp.exp(scores_of(piece, keys[:reach], start) - log)
        grad_shares = jnp.einsum("qkgd,tkd->kgqt", back, values[:reach], preferred_element_type=F32)
        center = jnp.sum(grad_shares * shares, axis=-1, keepdims=True)
        grad_raw = (shares * (grad_shares - center) * SCALE).astype(BF16)
        grad_piece = jnp.einsum("kgqt,tkd->qkgd", grad_raw, keys[:reach], preferred_element_type=F32)
        grad_queries.append(grad_piece.reshape(256, 8, HEAD_DIM))
        grad_keys = grad_keys.at[:reach].add(
            jnp.einsum("kgqt,qkgd->tkd", grad_raw, piece, preferred_element_type=F32)
        )
        grad_values = grad_values.at[:reach].add(
            jnp.einsum("kgqt,qkgd->tkd", shares.astype(BF16), back, preferred_element_type=F32)
        )
    return jnp.concatenate(grad_queries, axis=0), grad_keys, grad_values


def per_device(
    hidden_in, gain_attn, w_query, w_key, w_value, w_out, gain_mlp, w_gate, w_up, w_down, out_grad
):
    row, col = lax.axis_index("row"), lax.axis_index("col")
    w_att = jnp.concatenate([w_query, w_key, w_value, w_out], axis=1)
    tokens = jnp.stack([hidden_in, out_grad]).reshape(2, 2, 256, 768)
    gains = jnp.zeros((8, 768), F32).at[0].set(gain_attn).at[1].set(gain_mlp)
    att, gate_w, up_w, down_w, token_part, gain_part = gather_weights(
        w_att, w_gate, w_up, w_down, tokens, gains, 1
    )
    q_w, k_w, v_w = att[:, :768], att[:, 768:1152], att[:, 1152:1536]
    out_w = jnp.concatenate([att[:768, 1536:], att[768:, 1536:]], axis=1)
    mine = lax.dynamic_index_in_dim(tokens, col, 1, False)
    both = ordered(col, mine, token_part, 2)
    gain_all = ordered(col, gains[:2], gain_part[:2], 1)
    gain_attn, gain_mlp = gain_all[0], gain_all[1]
    resid, og_own = both[0].astype(F32), both[1]

    normed_attn, factor_attn, scaled_attn = norm_forward(resid, gain_attn)
    s1 = row_gather(scaled_attn, row, 2)
    places = jnp.arange(512) // 256 * 512 + col * 256 + jnp.arange(512) % 256
    cosine, sine = rotary(places)
    query = rotate(matmul(s1, q_w).reshape(512, 8, HEAD_DIM), cosine, sine).astype(BF16)
    keys = rotate(matmul(s1, k_w).reshape(512, 4, HEAD_DIM), cosine, sine).astype(BF16)
    values = matmul(s1, v_w).astype(BF16)
    keyval = jnp.concatenate([keys.reshape(512, 384), values], axis=1)
    keyval = ordered(
        col, keyval.reshape(2, 256, 768), exchange(keyval, "col", 3).reshape(2, 256, 768), 1
    ).reshape(1024, 768)
    keys, values = keyval[:, :384].reshape(1024, 4, HEAD_DIM), keyval[:, 384:].reshape(1024, 4, HEAD_DIM)
    attended, logs = attend(query, keys, values, col)
    attended = attended.astype(BF16)
    middle = resid + row_sum(matmul(attended, out_w), row, 4)
    normed_mlp, factor_mlp, scaled_mlp = norm_forward(middle, gain_mlp)
    s2 = row_gather(scaled_mlp, row, 2)
    gate, upper = matmul(s2, gate_w), matmul(s2, up_w)
    logistic = jax.nn.sigmoid(gate)
    activated = gate * logistic
    hidden = (activated * upper).astype(BF16)
    block_out = (middle + row_sum(matmul(hidden, down_w), row, 4)).astype(BF16)

    og = row_gather(og_own, row, 2)
    part_down = jnp.einsum("tf,tcd->cfd", hidden, og.reshape(512, 12, 128), preferred_element_type=F32)
    grad_hidden = inner_right(og, down_w)
    grad_gate = (grad_hidden * upper * logistic * (1.0 + gate * (1.0 - logistic))).astype(BF16)
    grad_upper = (grad_hidden * activated).astype(BF16)
    part_gate, part_up = inner_left(s2, grad_gate), inner_left(s2, grad_upper)
    grad_scaled_mlp = row_sum(inner_right(grad_gate, gate_w) + inner_right(grad_upper, up_w), row, 4)
    grad_norm, gain_mlp_part = norm_backward(grad_scaled_mlp, normed_mlp, factor_mlp, gain_mlp)
    grad_middle = og_own.astype(F32) + grad_norm
    gm = row_gather(grad_middle.astype(BF16), row, 2)
    part_out = inner_left(attended, gm)
    grad_attended = inner_right(gm, out_w).astype(BF16)
    grad_query, grad_keys, grad_values = attend_back(query, keys, values, grad_attended, logs, col)
    grad_kv = jnp.concatenate([grad_keys.reshape(1024, 384), grad_values.reshape(1024, 384)], axis=1)
    grad_kv = grad_kv.reshape(2, 2, 256, 768)
    kv_mine = lax.dynamic_index_in_dim(grad_kv, col, 1, False)
    kv_theirs = lax.dynamic_index_in_dim(grad_kv, 1 - col, 1, False).astype(BF16)
    grad_kv = (kv_mine + exchange(kv_theirs, "col", 5).astype(F32)).reshape(512, 768)
    grad_query = rotate(grad_query, cosine, -sine).reshape(512, 768).astype(BF16)
    grad_keys = rotate(grad_kv[:, :384].reshape(512, 4, HEAD_DIM), cosine, -sine).reshape(512, 384).astype(BF16)
    grad_values = grad_kv[:, 384:].astype(BF16)
    grad_qkv = jnp.concatenate([grad_query, grad_keys, grad_values], axis=1)
    part_qkv = inner_left(s1, grad_qkv)
    grad_scaled_attn = row_sum(inner_right(grad_qkv, att[:, :1536]), row, 4)
    grad_norm, gain_attn_part = norm_backward(grad_scaled_attn, normed_attn, factor_attn, gain_attn)
    in_grad = (grad_middle + grad_norm).astype(BF16)

    gain_parts = jnp.stack([gain_attn_part, gain_mlp_part])
    gain_parts = gain_parts + exchange(jnp.pad(gain_parts, ((0, 6), (0, 0))), "row", 6)[:2]
    gain_rows = gain_parts.reshape(2, 2, 6, 128).transpose(1, 2, 0, 3).reshape(2, 6, 1, 256)
    part_att = jnp.concatenate(
        [
            part_qkv.astype(BF16).reshape(2, 6, 128, 1536),
            part_out.astype(BF16).reshape(6, 128, 2, 768).transpose(2, 0, 1, 3),
            jnp.pad(gain_rows.astype(BF16), ((0, 0), (0, 0), (0, 127), (0, 0))),
        ],
        axis=3,
    )
    sum_down, sum_gate, sum_up, sum_att = sum_gradients(
        (
            part_down.astype(BF16).reshape(2, 6, 2048, 128),
            part_gate.astype(BF16).reshape(2, 6, 128, 2048),
            part_up.astype(BF16).reshape(2, 6, 128, 2048),
            part_att,
        ),
        7,
    )
    results = jnp.stack([block_out, in_grad]).reshape(2, 256, 2, 768)
    own = lax.dynamic_index_in_dim(results, col, 2, False)
    other = exchange(lax.dynamic_index_in_dim(results, 1 - col, 2, False), "col", 8)
    results = ordered(col, own, other, 1)
    att_rows = sum_att.reshape(768, 2560).astype(F32)
    gain_sums = sum_att[:, 0, 2304:].astype(F32)
    return (
        results[0],
        results[1],
        gain_sums[:, :128].reshape(768),
        att_rows[:, :768],
        att_rows[:, 768:1152],
        att_rows[:, 1152:1536],
        att_rows[:, 1536:2304],
        gain_sums[:, 128:].reshape(768),
        sum_gate.reshape(768, 2048).astype(F32),
        sum_up.reshape(768, 2048).astype(F32),
        sum_down.transpose(1, 0, 2).reshape(2048, 768).astype(F32),
    )


def solution(mesh):
    tokens, weight_in, weight_out, gain = P(("dp", "row"), "col"), P("col", "row"), P("row", "col"), P("col")
    return jax.shard_map(
        per_device,
        mesh=mesh,
        in_specs=(
            tokens, gain, weight_in, weight_in, weight_in, weight_out, gain, weight_in, weight_in, weight_out, tokens,
        ),
        out_specs=(
            tokens, tokens, gain, weight_in, weight_in, weight_in, weight_out, gain, weight_in, weight_in, weight_out,
        ),
        check_vma=False,
    )
```

```python
import functools
import math

import jax
import jax.numpy as jnp
import numpy as np
from jax import lax
from jax.experimental import pallas as pl
from jax.experimental.pallas import tpu as pltpu
from jax.sharding import PartitionSpec as P

MESH = pl.DeviceIdType.MESH
BF16 = jnp.bfloat16
F32 = jnp.float32
TYPES = 6
LANE_DIMS = ("xa", "xb", "za", "zb")
ALL_DIMS = ("xa", "xb", "ya", "yb", "za", "zb")


class Place:
    def __init__(self):
        dp = lax.axis_index("dp")
        self.row = lax.axis_index("row")
        self.col = lax.axis_index("col")
        self.x = dp % 4
        self.yh = (dp // 4) % 2
        self.z = dp // 8
        y = self.yh * 2 + self.col
        self.bit = {
            "xa": ((self.x + 1) // 2) % 2,
            "xb": self.x // 2,
            "ya": ((y + 1) // 2) % 2,
            "yb": y // 2,
            "za": ((self.z + 1) // 2) % 2,
            "zb": self.z // 2,
        }

    def partner(self, dim):
        x, yh, z, row, col = self.x, self.yh, self.z, self.row, self.col
        if dim == "xa":
            x = x + 1 - 2 * (x % 2)
        elif dim == "xb":
            x = 3 - x
        elif dim == "za":
            z = z + 1 - 2 * (z % 2)
        elif dim == "zb":
            z = 3 - z
        elif dim in ("ya", "col"):
            col = 1 - col
        elif dim == "yb":
            col = 1 - col
            yh = 1 - yh
        elif dim == "y2":
            yh = 1 - yh
        elif dim == "row":
            row = 1 - row
        return ((z * 2 + yh) * 4 + x, row, col)


def greet(place, dims):
    barrier = pltpu.get_barrier_semaphore()
    for dim in dims:
        pl.semaphore_signal(barrier, inc=1, device_id=place.partner(dim), device_id_type=MESH)
    pl.semaphore_wait(barrier, len(dims))


def remote(place, dim, src, dst, send_sem, recv_sem):
    return pltpu.make_async_remote_copy(
        src_ref=src,
        dst_ref=dst,
        send_sem=send_sem,
        recv_sem=recv_sem,
        device_id=place.partner(dim),
        device_id_type=MESH,
    )


def exchange(value, dim, ident):
    def kernel(src, dst, send_sem, recv_sem):
        place = Place()
        greet(place, (dim,))
        copy = remote(place, dim, src, dst, send_sem, recv_sem)
        copy.start()
        copy.wait()

    return pl.pallas_call(
        kernel,
        out_shape=jax.ShapeDtypeStruct(value.shape, value.dtype),
        in_specs=[pl.BlockSpec(memory_space=pl.ANY)],
        out_specs=pl.BlockSpec(memory_space=pl.ANY),
        scratch_shapes=[pltpu.SemaphoreType.DMA, pltpu.SemaphoreType.DMA],
        compiler_params=pltpu.CompilerParams(collective_id=ident, has_side_effects=True),
        name="exchange_" + dim,
    )(value)


def span(kind, width, fixed):
    if kind == "tall":
        start, size = 0, width
        for bit in fixed:
            size //= 2
            start = start + bit * size
        return pl.ds(pl.multiple_of(start, 16) if fixed else 0, size), pl.ds(0, 128)
    rows, cols, row_start, col_start = 128, width, 0, 0
    for index, bit in enumerate(fixed):
        if index < 3:
            rows //= 2
            row_start = row_start + bit * rows
        else:
            cols //= 2
            col_start = col_start + bit * cols
    if len(fixed) > 0:
        row_start = pl.multiple_of(row_start, 16)
    if len(fixed) > 3:
        col_start = pl.multiple_of(col_start, 128)
    return pl.ds(row_start, rows), pl.ds(col_start, cols)


GATHER_ORDERS = (
    ("xa", "xb", "za", "zb"),
    ("xb", "xa", "zb", "za"),
    ("za", "zb", "xa", "xb"),
    ("zb", "za", "xb", "xa"),
)


class WeightGather:
    def __init__(self, place, kind, width, source, target, send_sem, recv_sem):
        self.place, self.kind, self.width = place, kind, width
        self.source, self.target = source, target
        self.send_sem, self.recv_sem = send_sem, recv_sem

    def part(self, ref, chunk, fixed):
        rows, cols = span(self.kind, self.width, fixed)
        if self.kind == "tall":
            return ref.at[rows, pl.ds(chunk * 128, 128)]
        return ref.at[pl.ds(pl.multiple_of(chunk * 128 + rows.start, 16), rows.size), cols]

    def copy(self, chunk, step):
        place = self.place
        sems = (self.send_sem.at[chunk, step], self.recv_sem.at[chunk, step])
        if chunk >= 4:
            dim = "ya" if chunk == 4 else "yb"
            return remote(place, dim, self.part(self.source, chunk, ()), self.part(self.target, chunk, ()), *sems)
        order = GATHER_ORDERS[chunk]
        bits = [place.bit[dim] for dim in reversed(order)]
        if step == 0:
            dim = "ya" if chunk < 2 else "yb"
            return remote(place, dim, self.part(self.source, chunk, bits), self.part(self.target, chunk, bits), *sems)
        bits = bits[: 5 - step]
        part = self.part(self.target, chunk, bits)
        return remote(place, order[step - 1], part, part, *sems)

    def begin(self, chunks):
        for chunk in chunks:
            self.copy(chunk, 0).start()

    def advance(self, step):
        for chunk in range(4):
            self.copy(chunk, step - 1).wait_recv()
            self.copy(chunk, step).start()

    def finish(self):
        for chunk in range(TYPES):
            self.copy(chunk, 4 if chunk < 4 else 0).wait_recv()

    def drain(self):
        for chunk in range(TYPES):
            for step in range(5 if chunk < 4 else 1):
                self.copy(chunk, step).wait_send()


SUM_ORDERS = (
    ("xa", "xb", "ya", "yb", "za", "zb"),
    ("xb", "xa", "yb", "ya", "zb", "za"),
    ("ya", "yb", "za", "zb", "xa", "xb"),
    ("yb", "ya", "zb", "za", "xb", "xa"),
    ("za", "zb", "xa", "xb", "ya", "yb"),
    ("zb", "za", "xb", "xa", "yb", "ya"),
)
ALL_HALVES = pl.ds(0, 2)


class GradSum:
    def __init__(self, place, width, held, landing, stage, out, sems):
        self.place, self.kind, self.width = place, "wide", width
        self.held, self.landing, self.stage, self.out = held, landing, stage, out
        self.send_sem, self.recv_sem, self.ag_send, self.ag_recv, self.own_sem, self.stage_sem = sems

    def view(self, ref, half, chunk, fixed):
        rows, cols = span(self.kind, self.width, fixed)
        return ref.at[half, chunk, rows, cols]

    def moves(self, chunk, step):
        place = self.place
        order = SUM_ORDERS[chunk]
        dim = order[step]
        regular = [d for d in order if d != "ya"]
        p, q, c = place.bit["ya"], place.bit["yb"], place.col
        y_at = [i for i, d in enumerate(order) if d[0] == "y"]
        a_first = order[y_at[0]] == "ya"
        own = [place.bit[d] for d in order[:step] if d != "ya"]
        flipped = [1 - bit for bit in own]
        if dim[0] != "y":
            bit = place.bit[dim]
            if step < y_at[0]:
                half_own = half_land = ALL_HALVES
            else:
                half_own = c
                half_land = c if a_first else 1 - c
            sent = [(half_own, own + [1 - bit])]
            lands = [(half_land, flipped + [1 - bit])]
            kept = [(half_own, own + [bit])]
            landed = [(half_land, flipped + [bit])]
            return dim, sent, lands, kept, landed
        if a_first and dim == "ya":
            sent = [(1 - p, own + [0]), (p, own + [1])]
            lands = [(1 - p, flipped + [0]), (p, flipped + [1])]
            kept = [(p, own + [0]), (1 - p, own + [1])]
            landed = [(p, flipped + [0]), (1 - p, flipped + [1])]
        elif a_first:
            send_half = (p + 1 - q) % 2
            sent = [(send_half, own + [1 - q])]
            lands = [(c, flipped + [1 - q])]
            kept = [(c, own + [q])]
            landed = [(1 - c, flipped + [q])]
        elif dim == "yb":
            sent = [(ALL_HALVES, own + [1 - q])]
            lands = [(ALL_HALVES, flipped + [1 - q])]
            kept = [(ALL_HALVES, own + [q])]
            landed = [(ALL_HALVES, flipped + [q])]
        else:
            sent = [(1 - c, own)]
            lands = [(1 - c, flipped)]
            kept = [(c, own)]
            landed = [(c, flipped)]
        return dim, sent, lands, kept, landed

    def sends(self, chunk, step):
        dim, sent, lands, _, _ = self.moves(chunk, step)
        return [
            remote(
                self.place,
                dim,
                self.view(self.held, *region),
                self.view(self.landing, *there),
                self.send_sem.at[chunk, step, index],
                self.recv_sem.at[chunk, step, index],
            )
            for index, (region, there) in enumerate(zip(
                [(h, chunk, b) for h, b in sent], [(h, chunk, b) for h, b in lands]
            ))
        ]

    def start(self, step):
        for chunk in range(TYPES):
            for copy in self.sends(chunk, step):
                copy.start()

    def staged(self, chunk, step):
        _, _, _, kept, landed = self.moves(chunk, step)
        copies = []
        for index, ((half, bits), (from_half, from_bits)) in enumerate(zip(kept, landed)):
            rows, cols = span(self.kind, self.width, bits)
            halves = pl.ds(0, 2) if half is ALL_HALVES else index
            target = self.stage.at[chunk, halves, pl.ds(0, rows.size), pl.ds(0, cols.size)]
            source = self.view(self.landing, from_half, chunk, from_bits)
            copies.append(pltpu.make_async_copy(source, target, self.stage_sem.at[chunk, index]))
        return copies

    def add(self, step):
        for chunk in range(TYPES):
            for copy in self.sends(chunk, step):
                copy.wait_recv()
            for copy in self.staged(chunk, step):
                copy.start()
        for chunk in range(TYPES):
            for copy in self.staged(chunk, step):
                copy.wait()
            _, _, _, kept, _ = self.moves(chunk, step)
            for index, (half, bits) in enumerate(kept):
                rows, cols = span(self.kind, self.width, bits)
                for h in range(2 if half is ALL_HALVES else 1):
                    here = h if half is ALL_HALVES else half
                    there = h if half is ALL_HALVES else index

                    def body(i, carry, here=here, there=there, rows=rows, cols=cols, chunk=chunk):
                        at = pl.multiple_of(i * 16, 16)
                        mine = (here, chunk, pl.ds(pl.multiple_of(rows.start + at, 16), 16), cols)
                        came = (chunk, there, pl.ds(at, 16), pl.ds(0, cols.size))
                        self.held[mine] = self.held[mine] + self.stage[came]
                        return carry

                    lax.fori_loop(0, rows.size // 16, body, 0)
            if step < 5:
                for copy in self.sends(chunk, step + 1):
                    copy.start()


    def spread(self, chunk, step):
        place = self.place
        order = SUM_ORDERS[chunk]
        stages = []
        for d in reversed(order):
            if d[0] == "y":
                if "y2" not in stages:
                    stages.append("y2")
            else:
                stages.append(d)
        dim = stages[step]
        keep = [d for d in order if d != "ya"]
        done = set(stages[:step])
        bits = [place.bit[d] for d in keep if ("y2" if d == "yb" else d) not in done]
        rows, cols = span(self.kind, self.width, bits)
        target = self.out.at[chunk, rows, cols]
        source = self.held.at[place.col, chunk, rows, cols] if step == 0 else target
        return remote(place, dim, source, target, self.ag_send.at[chunk, step], self.ag_recv.at[chunk, step])

    def own(self, chunk):
        place = self.place
        bits = [place.bit[d] for d in SUM_ORDERS[chunk] if d != "ya"]
        rows, cols = span(self.kind, self.width, bits)
        return pltpu.make_async_copy(
            self.held.at[place.col, chunk, rows, cols], self.out.at[chunk, rows, cols], self.own_sem.at[chunk]
        )

    def spread_start(self):
        for chunk in range(TYPES):
            self.spread(chunk, 0).start()
            self.own(chunk).start()

    def spread_next(self, step):
        for chunk in range(TYPES):
            if step == 1:
                self.own(chunk).wait()
            self.spread(chunk, step - 1).wait_recv()
            self.spread(chunk, step).start()

    def finish(self):
        for chunk in range(TYPES):
            self.spread(chunk, 4).wait_recv()

    def release(self):
        for chunk in range(TYPES):
            for step in range(6):
                for copy in self.sends(chunk, step):
                    copy.wait_send()
            self.spread(chunk, 0).wait_send()

    def drain(self):
        for chunk in range(TYPES):
            for step in range(1, 5):
                self.spread(chunk, step).wait_send()


HEAD_DIM = 96
EPS = 1e-05
ROPE_BASE = 100000.0
NEG = -1e30
SCALE = 1.0 / math.sqrt(HEAD_DIM)
ANYWHERE = pl.BlockSpec(memory_space=pl.ANY)


def matmul(left, right):
    return jnp.dot(left, right, preferred_element_type=F32)


def inner_left(left, right):
    return lax.dot_general(left, right, (((0,), (0,)), ((), ())), preferred_element_type=F32)


def inner_right(left, right):
    return lax.dot_general(left, right, (((1,), (1,)), ((), ())), preferred_element_type=F32)


def rotary_tables():
    places = np.stack([np.concatenate([c * 256 + np.arange(256), 512 + c * 256 + np.arange(256)]) for c in range(2)])
    rates = ROPE_BASE ** (-2.0 * np.arange(HEAD_DIM // 2) / HEAD_DIM)
    angle = places[:, :, None] * rates[None, None, :]
    cosine, sine = np.cos(angle), np.sin(angle)
    return (
        np.tile(np.concatenate([cosine, cosine], axis=2), (1, 1, 4)).astype(np.float32),
        np.tile(np.concatenate([-sine, sine], axis=2), (1, 1, 4)).astype(np.float32),
    )


def swap_halves(value):
    half = HEAD_DIM // 2
    parts = []
    for head in range(value.shape[1] // HEAD_DIM):
        at = head * HEAD_DIM
        parts += [value[:, at + half : at + HEAD_DIM], value[:, at : at + half]]
    return jnp.concatenate(parts, axis=1)


def pad_head(value):
    return jnp.concatenate([value, jnp.zeros((value.shape[0], 128 - HEAD_DIM), value.dtype)], axis=1)


def aligned(start, size, step):
    return pl.ds(pl.multiple_of(start, step), size)


def split_key_values(source, own_col, kh, vh):
    for part in range(2):
        rows = aligned(part * 512 + own_col * 256, 256, 256)
        for head in range(4):
            at = head * HEAD_DIM
            kh[head, rows] = pad_head(source[part * 256 : part * 256 + 256, at : at + HEAD_DIM])
            vh[head, rows] = pad_head(source[part * 256 : part * 256 + 256, 384 + at : 384 + at + HEAD_DIM])


def masked_scores(query, keys, start):
    raw = inner_right(query, keys) * SCALE
    place = start + lax.broadcasted_iota(jnp.int32, raw.shape, 0)
    return jnp.where(lax.broadcasted_iota(jnp.int32, raw.shape, 1) <= place, raw, NEG)


FORWARD_KEEPS = (
    ("gains", (8, 1536), F32),
    ("x", (256, 1536), BF16),
    ("s1", (512, 1536), BF16),
    ("og", (512, 1536), BF16),
    ("qh", (8, 512, 128), BF16),
    ("kh", (4, 1024, 128), BF16),
    ("vh", (4, 1024, 128), BF16),
    ("attended", (512, 768), BF16),
    ("middle", (256, 1536), F32),
    ("s2", (512, 1536), BF16),
    ("hidden", (512, 2048), BF16),
    ("slope", (512, 2048), BF16),
    ("active", (512, 2048), BF16),
)
WEIGHTS = (("wide", 2304), ("wide", 2048), ("wide", 2048), ("tall", 2048))


def weight_shape(kind, width):
    return (width, 768) if kind == "tall" else (768, width)


def forward(w_att, w_gate, w_up, w_down, hidden_in, out_grad, gains, cosine, sine, ident):
    keeps = len(FORWARD_KEEPS)

    def kernel(*refs):
        sources, (hid, ogr, gain, cos_t, sin_t) = refs[:4], refs[4:9]
        others, bo_out, kept_out = refs[9:13], refs[13], refs[14 : 14 + keeps]
        refs = refs[14 + keeps :]
        v = {name: ref for (name, _, _), ref in zip(FORWARD_KEEPS, refs[:keeps])}
        (att_v, gate_v, up_v, down_v, cos_v, sin_v, kvc, kvo, oh, outgo, came1, came2, bo_v, send_sem, recv_sem, small_send,
         small_recv, local_sem, load_sem, keep_sem) = refs[keeps:]
        place = Place()
        row, col = place.row, place.col
        greet(place, ALL_DIMS + ("row",))
        own_cols = aligned(col * 768, 768, 128)
        their_cols = aligned((1 - col) * 768, 768, 128)
        own_rows = aligned(row * 256, 256, 256)
        their_rows = aligned((1 - row) * 256, 256, 256)
        mine = aligned(col * 256, 256, 256)
        theirs = aligned((1 - col) * 256, 256, 256)

        def small(index, dim, src, dst):
            return remote(place, dim, src, dst, small_send.at[index], small_recv.at[index])

        def local(index, src, dst):
            return pltpu.make_async_copy(src, dst, local_sem.at[index])

        keep_order = [name for name, _, _ in FORWARD_KEEPS]

        def keep(name):
            index = keep_order.index(name)
            return pltpu.make_async_copy(v[name], kept_out[index], keep_sem.at[index])

        x_move = small(0, "ya", hid.at[theirs], v["x"].at[:, own_cols])
        gain_move = small(1, "ya", gain, v["gains"].at[:, own_cols])
        og_move = small(2, "ya", ogr.at[theirs], v["og"].at[own_rows, own_cols])
        for copy in (x_move, gain_move):
            copy.start()
        jobs = [
            WeightGather(place, kind, width, source, other, send_sem.at[index], recv_sem.at[index])
            for index, ((kind, width), source, other) in enumerate(zip(WEIGHTS, sources, others))
        ]
        att, gate_j, up_j, down_j = jobs
        mlp = (gate_j, up_j, down_j)
        att.begin(range(6))
        og_move.start()
        for job in mlp:
            job.begin(range(4))
        x_load = local(0, hid.at[mine], v["x"].at[:, own_cols])
        gain_load = local(1, gain, v["gains"].at[:, own_cols])
        og_load = local(2, ogr.at[mine], v["og"].at[own_rows, own_cols])
        cos_load = local(3, cos_t.at[col], cos_v)
        sin_load = local(4, sin_t.at[col], sin_v)
        for copy in (x_load, gain_load, og_load, cos_load, sin_load):
            copy.start()
        whole = (att_v, gate_v, up_v, down_v)
        own_loads, other_loads = [], []
        for index, ((kind, _), source, other, target) in enumerate(zip(WEIGHTS, sources, others, whole)):
            tall = kind == "tall"
            own_loads.append(
                pltpu.make_async_copy(
                    source, target.at[:, own_cols] if tall else target.at[own_cols], load_sem.at[0, index]
                )
            )
            other_loads.append(
                pltpu.make_async_copy(
                    other, target.at[:, their_cols] if tall else target.at[their_cols], load_sem.at[1, index]
                )
            )
        for copy in own_loads:
            copy.start()

        x_load.wait()
        gain_load.wait()
        x_move.wait_recv()
        gain_move.wait_recv()

        def norm_into(read, gain_row, target):
            def block(i, carry):
                value = read(i)
                factor = lax.rsqrt(jnp.mean(value * value, axis=1, keepdims=True) + EPS)
                target[aligned(row * 256 + i * 64, 64, 64)] = (
                    value * factor * v["gains"][gain_row : gain_row + 1, :]
                ).astype(BF16)
                return carry

            lax.fori_loop(0, 4, block, 0)

        norm_into(lambda i: v["x"][aligned(i * 64, 64, 64)].astype(F32), 0, v["s1"])
        keep("x").start()
        keep("gains").start()
        s1_move = small(3, "row", v["s1"].at[own_rows], v["s1"].at[own_rows])
        s1_move.start()
        att.advance(1)
        att.advance(2)
        for job in mlp:
            job.begin(range(4, 6))
        att.advance(3)
        for job in mlp:
            job.advance(1)
        att.advance(4)
        s1_move.wait_recv()
        cos_load.wait()
        sin_load.wait()
        keep("s1").start()
        own_loads[0].wait()
        att.finish()
        other_loads[0].start()
        for job in mlp:
            job.advance(2)
        other_loads[0].wait()

        def project(at):
            return matmul(v["s1"][...], att_v[:, at : at + 384])

        def turned(value):
            return (value * cos_v[...] + swap_halves(value) * sin_v[...]).astype(BF16)

        kvc[:, 0:384] = turned(project(768))
        kvc[:, 384:768] = project(1152).astype(BF16)
        kv_move = small(4, "ya", kvc, kvo)
        kv_move.start()
        for part in range(2):
            value = turned(project(part * 384))
            for head in range(4):
                v["qh"][part * 4 + head] = pad_head(value[:, head * HEAD_DIM : (head + 1) * HEAD_DIM])
        split_key_values(kvc, col, v["kh"], v["vh"])
        keep("qh").start()
        for job in mlp:
            job.advance(3)
        kv_move.wait_recv()
        split_key_values(kvo, 1 - col, v["kh"], v["vh"])
        keep("kh").start()
        keep("vh").start()

        def heads(h, carry):
            for pair in range(2):
                for at, reach in ((0, 512), (256, 1024)):
                    scores = masked_scores(
                        v["qh"][h * 2 + pair, at : at + 256], v["kh"][h, 0:reach], at * 2 + col * 256
                    )
                    powers = jnp.exp(scores - jnp.max(scores, axis=1, keepdims=True))
                    total = jnp.sum(powers, axis=1, keepdims=True)
                    shares = (powers * (1.0 / total)).astype(BF16)
                    oh[h * 2 + pair, at : at + 256] = matmul(shares, v["vh"][h, 0:reach]).astype(BF16)
            return carry

        lax.fori_loop(0, 4, heads, 0)
        for job in mlp:
            job.advance(4)
        v["attended"][...] = jnp.concatenate([oh[j][:, 0:HEAD_DIM] for j in range(8)], axis=1)
        keep("attended").start()

        def summed(index, read, weight, came, done):
            def half(rows, put):
                left = read(rows)
                for h in range(3):
                    put(h, matmul(left, weight(h)))

            def put_out(h, value):
                outgo[:, h * 512 : h * 512 + 512] = value

            half(their_rows, put_out)
            move = small(index, "row", outgo, came)
            move.start()
            half(own_rows, done)
            move.wait_recv()
            return move

        def out_weight(h):
            if h == 0:
                return att_v[0:768, 1536 : 1536 + 512]
            if h == 2:
                return att_v[768:1536, 1536 + 256 : 2304]
            return jnp.concatenate([att_v[0:768, 2048:2304], att_v[768:1536, 1536:1792]], axis=1)

        def add_middle(h, value):
            at = h * 512
            v["middle"][:, at : at + 512] = v["x"][:, at : at + 512].astype(F32) + value

        out_move = summed(5, lambda rows: v["attended"][rows], out_weight, came1, add_middle)
        v["middle"][...] = v["middle"][...] + came1[...]
        keep("middle").start()
        norm_into(lambda i: v["middle"][aligned(i * 64, 64, 64)], 1, v["s2"])
        s2_move = small(6, "row", v["s2"].at[own_rows], v["s2"].at[own_rows])
        s2_move.start()
        og_load.wait()
        og_move.wait_recv()
        og_swap = small(7, "row", v["og"].at[own_rows], v["og"].at[own_rows])
        og_swap.start()
        for index, job in ((1, gate_j), (2, up_j)):
            own_loads[index].wait()
            job.finish()
            other_loads[index].start()
        s2_move.wait_recv()
        keep("s2").start()
        og_swap.wait_recv()
        keep("og").start()
        other_loads[1].wait()
        other_loads[2].wait()

        def units(n, carry):
            cols = aligned(n * 256, 256, 256)
            gate = matmul(v["s2"][...], gate_v[:, cols])
            upper = matmul(v["s2"][...], up_v[:, cols])
            logistic = 1.0 / (1.0 + jnp.exp(-gate))
            active = gate * logistic
            v["hidden"][:, cols] = (active * upper).astype(BF16)
            v["slope"][:, cols] = (upper * logistic * (1.0 + gate * (1.0 - logistic))).astype(BF16)
            v["active"][:, cols] = active.astype(BF16)
            return carry

        lax.fori_loop(0, 8, units, 0)
        for name in ("hidden", "slope", "active"):
            keep(name).start()
        own_loads[3].wait()
        down_j.finish()
        other_loads[3].start()
        out_move.wait_send()
        other_loads[3].wait()

        def add_out(h, value):
            at = h * 512
            came1[:, at : at + 512] = v["middle"][:, at : at + 512] + value

        down_move = summed(
            8, lambda rows: v["hidden"][rows], lambda h: down_v[:, h * 512 : h * 512 + 512], came2, add_out
        )
        bo_v[...] = (came1[...] + came2[...]).astype(BF16)
        bo_move = small(9, "ya", bo_v.at[:, their_cols], bo_out.at[mine])
        bo_move.start()
        bo_own = local(5, bo_v.at[:, own_cols], bo_out.at[mine])
        bo_own.start()
        bo_own.wait()
        bo_move.wait()
        for job in jobs:
            job.drain()
        for copy in (x_move, gain_move, og_move, s1_move, kv_move, s2_move, og_swap, down_move):
            copy.wait_send()
        for name in keep_order:
            keep(name).wait()

    outs = [jax.ShapeDtypeStruct(weight_shape(*w), BF16) for w in WEIGHTS]
    outs += [jax.ShapeDtypeStruct((512, 768), BF16)]
    outs += [jax.ShapeDtypeStruct(shape, kind) for _, shape, kind in FORWARD_KEEPS]
    return pl.pallas_call(
        kernel,
        out_shape=outs,
        in_specs=[ANYWHERE] * 9,
        out_specs=[ANYWHERE] * (5 + keeps),
        scratch_shapes=[pltpu.VMEM(shape, kind) for _, shape, kind in FORWARD_KEEPS]
        + [
            pltpu.VMEM((1536, 2304), BF16),
            pltpu.VMEM((1536, 2048), BF16),
            pltpu.VMEM((1536, 2048), BF16),
            pltpu.VMEM((2048, 1536), BF16),
            pltpu.VMEM((512, 384), F32),
            pltpu.VMEM((512, 384), F32),
            pltpu.VMEM((512, 768), BF16),
            pltpu.VMEM((512, 768), BF16),
            pltpu.VMEM((8, 512, 128), BF16),
            pltpu.VMEM((256, 1536), F32),
            pltpu.VMEM((256, 1536), F32),
            pltpu.VMEM((256, 1536), F32),
            pltpu.VMEM((256, 1536), BF16),
            pltpu.SemaphoreType.DMA((4, TYPES, 5)),
            pltpu.SemaphoreType.DMA((4, TYPES, 5)),
            pltpu.SemaphoreType.DMA((10,)),
            pltpu.SemaphoreType.DMA((10,)),
            pltpu.SemaphoreType.DMA((6,)),
            pltpu.SemaphoreType.DMA((2, 4)),
            pltpu.SemaphoreType.DMA((keeps,)),
        ],
        compiler_params=pltpu.CompilerParams(
            collective_id=ident, has_side_effects=True, vmem_limit_bytes=62 << 20
        ),
        name="forward",
    )(w_att, w_gate, w_up, w_down, hidden_in, out_grad, gains, cosine, sine)


GROUP_WIDTHS = (2048, 2048, 2048, 2560)


def backward(own_weights, other_weights, kept, cosine, sine, ident):
    keeps = len(FORWARD_KEEPS)
    groups = len(GROUP_WIDTHS)
    names = [name for name, _, _ in FORWARD_KEEPS]

    def kernel(*refs):
        (w_att, _, _, w_down), (o_att, _, _, o_down) = refs[0:4], refs[4:8]
        (w_gate, w_up), (o_gate, o_up) = refs[1:3], refs[5:7]
        hbm = dict(zip(names, refs[8 : 8 + keeps]))
        cos_t, sin_t = refs[8 + keeps : 10 + keeps]
        refs = refs[10 + keeps :]
        sums, landing, ig_out = refs[:groups], refs[groups : 2 * groups], refs[2 * groups]
        (held0, held1, held2, stage, pool, og, units, slope, active, qh, kh, vh, doh, attended, dk, dv, kv_own, kv_out, kv_in,
         dqkv, cos_v, sin_v, outgo, mine_v, came1, came2, middle, x_v, gains, gain_sum, gain_came, ig_v,
         rs_send, rs_recv, ag_send, ag_recv, own_sem, stage_sem, load_sem, pool_sem, small_send, small_recv,
        ) = refs[2 * groups + 1 :]
        place = Place()
        row, col = place.row, place.col
        greet(place, ALL_DIMS + ("y2", "row"))
        own_cols = aligned(col * 768, 768, 128)
        their_cols = aligned((1 - col) * 768, 768, 128)
        own_rows = aligned(row * 256, 256, 256)
        their_rows = aligned((1 - row) * 256, 256, 256)
        mine = aligned(col * 256, 256, 256)

        def small(index, dim, src, dst):
            return remote(place, dim, src, dst, small_send.at[index], small_recv.at[index])

        held = (held0, held1, held2, held0)
        down, gate, up, att = [
            GradSum(
                place, width, held[g], landing[g], stage, sums[g],
                (rs_send.at[g], rs_recv.at[g], ag_send.at[g], ag_recv.at[g], own_sem.at[g], stage_sem),
            )
            for g, width in enumerate(GROUP_WIDTHS)
        ]
        loads = {}

        def load(name, source, target):
            copy = pltpu.make_async_copy(source, target, load_sem.at[len(loads)])
            copy.start()
            loads[name] = copy

        def down_tile(n):
            at = pl.ds(pl.multiple_of(1024 + (n % 2) * 256, 256), 256)
            rows = pl.ds(pl.multiple_of(n * 256, 256), 256)
            return [
                pltpu.make_async_copy(w_down.at[rows], pool.at[at, own_cols], pool_sem.at[n % 2, 0]),
                pltpu.make_async_copy(o_down.at[rows], pool.at[at, their_cols], pool_sem.at[n % 2, 1]),
            ]

        def expand_tile(n):
            sources = (w_gate, w_up) if n < 3 else (o_gate, o_up)
            rows = pl.ds((n % 3) * 256, 256)
            slot = n % 2
            return [
                pltpu.make_async_copy(
                    source.at[rows], pool.at[pl.ds((slot * 2 + k) * 256, 256)], pool_sem.at[2 + slot, k]
                )
                for k, source in enumerate(sources)
            ]

        load("og", hbm["og"], og)
        load("hidden", hbm["hidden"], units)
        for copy in down_tile(0):
            copy.start()
        load("slope", hbm["slope"], slope)
        load("active", hbm["active"], active)
        for n in range(2):
            for copy in expand_tile(n):
                copy.start()
        load("middle", hbm["middle"], middle)
        load("gains", hbm["gains"], gains)
        load("qh", hbm["qh"], qh)
        load("kh", hbm["kh"], kh)
        load("vh", hbm["vh"], vh)
        load("attended", hbm["attended"], attended)
        load("cos", cos_t.at[col], cos_v)
        load("sin", sin_t.at[col], sin_v)
        load("x", hbm["x"], x_v)

        def weight_grad(left, right, target, at, blocks, cols):
            def block(i, carry):
                half, pair = i // 3, i % 3
                lhs = left[:, aligned(i * 256, 256, 256)]
                for n in range(cols // 512):
                    value = inner_left(lhs, right[:, n * 512 : n * 512 + 512]).astype(BF16)
                    for k in range(2):
                        target[half, pair * 2 + k, :, at + n * 512 : at + n * 512 + 512] = value[k * 128 : k * 128 + 128]
                return carry

            lax.fori_loop(0, blocks, block, 0)

        loads["og"].wait()
        loads["hidden"].wait()
        weight_grad(og, units, held0, 0, 6, 2048)
        down.start(0)
        load("s2", hbm["s2"], units.at[:, pl.ds(0, 1536)])
        loads["slope"].wait()
        loads["active"].wait()

        def hidden_tile(n, carry):
            @pl.when(n < 7)
            def _():
                for copy in down_tile(n + 1):
                    copy.start()

            for copy in down_tile(n):
                copy.wait()
            weight = pool[pl.ds(pl.multiple_of(1024 + (n % 2) * 256, 256), 256), 0:1536]
            grad = inner_right(og[...], weight)
            cols = aligned(n * 256, 256, 256)
            slope[:, cols] = (grad * slope[:, cols].astype(F32)).astype(BF16)
            active[:, cols] = (grad * active[:, cols].astype(F32)).astype(BF16)
            return carry

        lax.fori_loop(0, 8, hidden_tile, 0)
        loads["s2"].wait()
        weight_grad(units, slope, held1, 0, 6, 2048)
        gate.start(0)
        down.add(0)
        weight_grad(units, active, held2, 0, 6, 2048)
        up.start(0)
        load("s1", hbm["s1"], units.at[:, pl.ds(0, 1536)])
        down.add(1)

        for n in range(6):
            for copy in expand_tile(n):
                copy.wait()
            slot = (n % 2) * 512
            cols = aligned((col if n < 3 else 1 - col) * 768 + (n % 3) * 256, 256, 256)
            for rows, target in ((their_rows, outgo), (own_rows, mine_v)):
                target[:, cols] = inner_right(slope[rows], pool[slot : slot + 256, :]) + inner_right(
                    active[rows], pool[slot + 256 : slot + 512, :]
                )
            if n + 2 < 6:
                for copy in expand_tile(n + 2):
                    copy.start()
            if n == 2:
                gate.add(0)
        mlp_move = small(0, "row", outgo, came1)
        mlp_move.start()
        load("out_own", w_att.at[:, pl.ds(1536, 768)], pool.at[pl.ds(0, 768), own_cols])
        load("out_other", o_att.at[:, pl.ds(1536, 768)], pool.at[pl.ds(0, 768), their_cols])
        down.add(2)
        loads["middle"].wait()
        loads["gains"].wait()
        mlp_move.wait_recv()

        def norm_back(value_of, grad_came, gain_row, finish):
            gain_sum[gain_row : gain_row + 1, :] = jnp.zeros((1, 1536), F32)

            def block(i, carry):
                rows = aligned(i * 32, 32, 32)
                value = value_of(rows)
                grad = mine_v[rows] + grad_came[rows]
                factor = lax.rsqrt(jnp.mean(value * value, axis=1, keepdims=True) + EPS)
                normed = value * factor
                gain_sum[gain_row : gain_row + 1, :] += jnp.sum(grad * normed, axis=0, keepdims=True)
                scaled = grad * gains[gain_row : gain_row + 1, :]
                back = factor * (scaled - normed * jnp.mean(scaled * normed, axis=1, keepdims=True))
                finish(i, rows, back)
                return carry

            lax.fori_loop(0, 8, block, 0)

        def put_middle(i, rows, back):
            at = aligned(row * 256 + i * 32, 32, 32)
            total = og[at].astype(F32) + back
            middle[rows] = total
            og[at] = total.astype(BF16)

        norm_back(lambda rows: middle[rows], came1, 1, put_middle)
        gm_move = small(1, "row", og.at[own_rows], og.at[own_rows])
        gm_move.start()
        loads["out_own"].wait()
        loads["out_other"].wait()
        gate.add(1)
        gm_move.wait_recv()

        for part in range(2):
            value = inner_right(og[...], pool[part * 384 : part * 384 + 384, 0:1536]).astype(BF16)
            for head in range(4):
                doh[part * 4 + head] = pad_head(value[:, head * HEAD_DIM : (head + 1) * HEAD_DIM])
        load("qkv_own", w_att.at[:, pl.ds(0, 1536)], pool.at[own_cols, pl.ds(0, 1536)])
        load("qkv_other", o_att.at[:, pl.ds(0, 1536)], pool.at[their_cols, pl.ds(0, 1536)])
        up.add(0)
        down.add(3)
        for name in ("qh", "kh", "vh", "cos", "sin"):
            loads[name].wait()

        def heads(h, carry):
            dk[...] = jnp.zeros((1024, 128), F32)
            dv[...] = jnp.zeros((1024, 128), F32)
            for pair in range(2):
                for at, reach in ((0, 512), (256, 1024)):
                    rows = slice(at, at + 256)
                    query, grad = qh[h * 2 + pair, rows], doh[h * 2 + pair, rows]
                    keys, values = kh[h, 0:reach], vh[h, 0:reach]
                    scores = masked_scores(query, keys, at * 2 + col * 256)
                    powers = jnp.exp(scores - jnp.max(scores, axis=1, keepdims=True))
                    shares = powers * (1.0 / jnp.sum(powers, axis=1, keepdims=True))
                    grad_shares = inner_right(grad, values)
                    center = jnp.sum(grad_shares * shares, axis=1, keepdims=True)
                    grad_raw = (shares * (grad_shares - center) * SCALE).astype(BF16)
                    dk[0:reach] += inner_left(grad_raw, query)
                    dv[0:reach] += inner_left(shares.astype(BF16), grad)
                    value = matmul(grad_raw, keys)[:, 0:HEAD_DIM]
                    value = value * cos_v[rows, 0:HEAD_DIM] - swap_halves(value) * sin_v[rows, 0:HEAD_DIM]
                    qh[h * 2 + pair, rows] = pad_head(value.astype(BF16))
            kh[h] = dk[...].astype(BF16)
            vh[h] = dv[...].astype(BF16)
            return carry

        lax.fori_loop(0, 2, heads, 0)
        gate.add(2)
        up.add(1)
        down.add(4)
        lax.fori_loop(2, 4, heads, 0)

        def packed(own_col, part):
            rows = aligned(part * 512 + own_col * 256, 256, 256)
            return jnp.concatenate(
                [kh[h, rows][:, 0:HEAD_DIM] for h in range(4)] + [vh[h, rows][:, 0:HEAD_DIM] for h in range(4)], axis=1
            )

        for part in range(2):
            kv_out[part * 256 : part * 256 + 256] = packed(1 - col, part)
        kv_move = small(2, "ya", kv_out, kv_in)
        kv_move.start()
        for part in range(2):
            kv_own[part * 256 : part * 256 + 256] = packed(col, part)
        dqkv[:, 0:768] = jnp.concatenate([qh[j][:, 0:HEAD_DIM] for j in range(8)], axis=1)
        down.add(5)
        down.spread_start()
        gate.add(3)
        up.add(2)
        down.spread_next(1)
        kv_move.wait_recv()
        total = kv_own[:, 0:384].astype(F32) + kv_in[:, 0:384].astype(F32)
        dqkv[:, 768:1152] = (total * cos_v[...] - swap_halves(total) * sin_v[...]).astype(BF16)
        dqkv[:, 1152:1536] = (kv_own[:, 384:768].astype(F32) + kv_in[:, 384:768].astype(F32)).astype(BF16)
        loads["qkv_own"].wait()
        loads["qkv_other"].wait()
        mlp_move.wait_send()
        for n in range(3):
            cols = slice(n * 512, n * 512 + 512)
            for rows, target in ((their_rows, outgo), (own_rows, mine_v)):
                target[:, cols] = inner_right(dqkv[rows], pool[cols, 0:1536])
        att_move = small(3, "row", outgo, came2)
        att_move.start()
        gate.add(4)
        up.add(3)
        down.release()
        loads["x"].wait()
        loads["s1"].wait()
        loads["attended"].wait()
        att_move.wait_recv()

        def put_input(i, rows, back):
            ig_v[rows] = (middle[rows] + back).astype(BF16)

        norm_back(lambda rows: x_v[rows].astype(F32), came2, 0, put_input)
        gain_move = small(4, "row", gain_sum, gain_came)
        gain_move.start()
        ig_move = small(5, "ya", ig_v.at[:, their_cols], ig_out.at[mine])
        ig_move.start()
        ig_own = pltpu.make_async_copy(ig_v.at[:, own_cols], ig_out.at[mine], load_sem.at[len(loads)])
        ig_own.start()
        weight_grad(units, dqkv, held0, 0, 6, 1536)

        def out_grads(i, carry):
            lhs = attended[:, aligned(i * 256, 256, 256)]
            for half in range(2):
                value = inner_left(lhs, og[:, half * 768 : half * 768 + 768]).astype(BF16)
                for k in range(2):
                    held0[half, i * 2 + k, :, 1536:2304] = value[k * 128 : k * 128 + 128]
            return carry

        lax.fori_loop(0, 3, out_grads, 0)
        gain_move.wait_recv()
        for half in range(2):
            for chunk in range(TYPES):
                at = half * 768 + chunk * 128
                for k in range(2):
                    total = gain_sum[k : k + 1, at : at + 128] + gain_came[k : k + 1, at : at + 128]
                    first = lax.broadcasted_iota(jnp.int32, (16, 128), 0) == 0
                    lanes = slice(2304 + k * 128, 2304 + k * 128 + 128)
                    held0[half, chunk, 0:16, lanes] = jnp.where(first, total, 0.0).astype(BF16)
                    held0[half, chunk, 16:128, lanes] = jnp.zeros((112, 128), BF16)
        att.start(0)

        gate.add(5)
        gate.spread_start()
        up.add(4)
        down.spread_next(2)
        up.add(5)
        up.spread_start()
        gate.spread_next(1)
        down.spread_next(3)
        att.add(0)
        up.spread_next(1)
        gate.spread_next(2)
        att.add(1)
        att.add(2)
        down.spread_next(4)
        up.spread_next(2)
        att.add(3)
        gate.spread_next(3)
        att.add(4)
        att.add(5)
        att.spread_start()
        up.spread_next(3)
        gate.spread_next(4)
        att.spread_next(1)
        att.spread_next(2)
        up.spread_next(4)
        att.spread_next(3)
        att.spread_next(4)
        for job in (down, gate, up, att):
            job.finish()
        ig_own.wait()
        for copy in (gm_move, kv_move, att_move, gain_move):
            copy.wait_send()
        ig_move.wait()
        for job in (gate, up, att):
            job.release()
        for job in (down, gate, up, att):
            job.drain()

    chunk_shapes = [(TYPES, 128, width) for width in GROUP_WIDTHS]
    outs = [jax.ShapeDtypeStruct(shape, BF16) for shape in chunk_shapes]
    outs += [jax.ShapeDtypeStruct((2,) + shape, BF16) for shape in chunk_shapes]
    outs += [jax.ShapeDtypeStruct((512, 768), BF16)]
    dma = pltpu.SemaphoreType.DMA
    return pl.pallas_call(
        kernel,
        out_shape=outs,
        in_specs=[ANYWHERE] * (10 + keeps),
        out_specs=[ANYWHERE] * len(outs),
        scratch_shapes=[
            pltpu.VMEM((2, TYPES, 128, 2560), BF16),
            pltpu.VMEM((2, TYPES, 128, 2048), BF16),
            pltpu.VMEM((2, TYPES, 128, 2048), BF16),
            pltpu.VMEM((TYPES, 2, 64, 2560), BF16),
            pltpu.VMEM((1536, 2048), BF16),
            pltpu.VMEM((512, 1536), BF16),
            pltpu.VMEM((512, 2048), BF16),
            pltpu.VMEM((512, 2048), BF16),
            pltpu.VMEM((512, 2048), BF16),
            pltpu.VMEM((8, 512, 128), BF16),
            pltpu.VMEM((4, 1024, 128), BF16),
            pltpu.VMEM((4, 1024, 128), BF16),
            pltpu.VMEM((8, 512, 128), BF16),
            pltpu.VMEM((512, 768), BF16),
            pltpu.VMEM((1024, 128), F32),
            pltpu.VMEM((1024, 128), F32),
            pltpu.VMEM((512, 768), BF16),
            pltpu.VMEM((512, 768), BF16),
            pltpu.VMEM((512, 768), BF16),
            pltpu.VMEM((512, 1536), BF16),
            pltpu.VMEM((512, 384), F32),
            pltpu.VMEM((512, 384), F32),
            pltpu.VMEM((256, 1536), F32),
            pltpu.VMEM((256, 1536), F32),
            pltpu.VMEM((256, 1536), F32),
            pltpu.VMEM((256, 1536), F32),
            pltpu.VMEM((256, 1536), F32),
            pltpu.VMEM((256, 1536), BF16),
            pltpu.VMEM((8, 1536), F32),
            pltpu.VMEM((8, 1536), F32),
            pltpu.VMEM((8, 1536), F32),
            pltpu.VMEM((256, 1536), BF16),
            dma((groups, TYPES, 6, 2)),
            dma((groups, TYPES, 6, 2)),
            dma((groups, TYPES, 5)),
            dma((groups, TYPES, 5)),
            dma((groups, TYPES)),
            dma((TYPES, 2)),
            dma((24,)),
            dma((4, 2)),
            dma((6,)),
            dma((6,)),
        ],
        compiler_params=pltpu.CompilerParams(
            collective_id=ident, has_side_effects=True, vmem_limit_bytes=63 << 20
        ),
        name="backward",
    )(*own_weights, *other_weights, *kept, cosine, sine)


def per_device(
    hidden_in, gain_attn, w_query, w_key, w_value, w_out, gain_mlp, w_gate, w_up, w_down, out_grad
):
    w_att = jnp.concatenate([w_query, w_key, w_value, w_out], axis=1)
    gains = jnp.concatenate([gain_attn[None], gain_mlp[None], jnp.zeros((6, 768), F32)], axis=0)
    cosine, sine = (jnp.asarray(table) for table in rotary_tables())
    done = forward(w_att, w_gate, w_up, w_down, hidden_in, out_grad, gains, cosine, sine, 1)
    others, block_out, kept = done[:4], done[4], done[5:]
    back = backward((w_att, w_gate, w_up, w_down), others, kept, cosine, sine, 2)
    sum_down, sum_gate, sum_up, sum_att = back[:4]
    att_rows = sum_att.reshape(768, 2560)
    gain_sums = sum_att[:, 0, 2304:].astype(F32)
    return (
        block_out,
        back[8],
        gain_sums[:, :128].reshape(768),
        att_rows[:, :768].astype(F32),
        att_rows[:, 768:1152].astype(F32),
        att_rows[:, 1152:1536].astype(F32),
        att_rows[:, 1536:2304].astype(F32),
        gain_sums[:, 128:].reshape(768),
        sum_gate.reshape(768, 2048).astype(F32),
        sum_up.reshape(768, 2048).astype(F32),
        sum_down.reshape(768, 2048).T.astype(F32),
    )


def solution(mesh):
    tokens, weight_in, weight_out, gain = P(("dp", "row"), "col"), P("col", "row"), P("row", "col"), P("col")
    return jax.shard_map(
        per_device,
        mesh=mesh,
        in_specs=(
            tokens, gain, weight_in, weight_in, weight_in, weight_out, gain, weight_in, weight_in, weight_out, tokens,
        ),
        out_specs=(
            tokens, tokens, gain, weight_in, weight_in, weight_in, weight_out, gain, weight_in, weight_in, weight_out,
        ),
        check_vma=False,
    )
```

```python
import functools
import math

import jax
import jax.numpy as jnp
import numpy as np
from jax import lax
from jax.experimental import pallas as pl
from jax.experimental.pallas import tpu as pltpu
from jax.sharding import PartitionSpec as P

MESH = pl.DeviceIdType.MESH
BF16 = jnp.bfloat16
F32 = jnp.float32
TYPES = 6
LANE_DIMS = ("xa", "xb", "za", "zb")
ALL_DIMS = ("xa", "xb", "ya", "yb", "za", "zb")


class Place:
    def __init__(self):
        dp = lax.axis_index("dp")
        self.row = lax.axis_index("row")
        self.col = lax.axis_index("col")
        self.x = dp % 4
        self.yh = (dp // 4) % 2
        self.z = dp // 8
        y = self.yh * 2 + self.col
        self.bit = {
            "xa": ((self.x + 1) // 2) % 2,
            "xb": self.x // 2,
            "ya": ((y + 1) // 2) % 2,
            "yb": y // 2,
            "za": ((self.z + 1) // 2) % 2,
            "zb": self.z // 2,
        }

    def partner(self, dim):
        x, yh, z, row, col = self.x, self.yh, self.z, self.row, self.col
        if dim == "xa":
            x = x + 1 - 2 * (x % 2)
        elif dim == "xb":
            x = 3 - x
        elif dim == "za":
            z = z + 1 - 2 * (z % 2)
        elif dim == "zb":
            z = 3 - z
        elif dim in ("ya", "col"):
            col = 1 - col
        elif dim == "yb":
            col = 1 - col
            yh = 1 - yh
        elif dim == "y2":
            yh = 1 - yh
        elif dim == "row":
            row = 1 - row
        return ((z * 2 + yh) * 4 + x, row, col)


def greet(place, dims):
    barrier = pltpu.get_barrier_semaphore()
    for dim in dims:
        pl.semaphore_signal(barrier, inc=1, device_id=place.partner(dim), device_id_type=MESH)
    pl.semaphore_wait(barrier, len(dims))


def remote(place, dim, src, dst, send_sem, recv_sem):
    return pltpu.make_async_remote_copy(
        src_ref=src,
        dst_ref=dst,
        send_sem=send_sem,
        recv_sem=recv_sem,
        device_id=place.partner(dim),
        device_id_type=MESH,
    )


def exchange(value, dim, ident):
    def kernel(src, dst, send_sem, recv_sem):
        place = Place()
        greet(place, (dim,))
        copy = remote(place, dim, src, dst, send_sem, recv_sem)
        copy.start()
        copy.wait()

    return pl.pallas_call(
        kernel,
        out_shape=jax.ShapeDtypeStruct(value.shape, value.dtype),
        in_specs=[pl.BlockSpec(memory_space=pl.ANY)],
        out_specs=pl.BlockSpec(memory_space=pl.ANY),
        scratch_shapes=[pltpu.SemaphoreType.DMA, pltpu.SemaphoreType.DMA],
        compiler_params=pltpu.CompilerParams(collective_id=ident, has_side_effects=True),
        name="exchange_" + dim,
    )(value)


def span(kind, width, fixed):
    if kind == "tall":
        start, size = 0, width
        for bit in fixed:
            size //= 2
            start = start + bit * size
        return pl.ds(pl.multiple_of(start, 16) if fixed else 0, size), pl.ds(0, 128)
    rows, cols, row_start, col_start = 128, width, 0, 0
    for index, bit in enumerate(fixed):
        if index < 3:
            rows //= 2
            row_start = row_start + bit * rows
        else:
            cols //= 2
            col_start = col_start + bit * cols
    if len(fixed) > 0:
        row_start = pl.multiple_of(row_start, 16)
    if len(fixed) > 3:
        col_start = pl.multiple_of(col_start, 128)
    return pl.ds(row_start, rows), pl.ds(col_start, cols)


GATHER_ORDERS = (
    ("xa", "xb", "za", "zb"),
    ("xb", "xa", "zb", "za"),
    ("za", "zb", "xa", "xb"),
    ("zb", "za", "xb", "xa"),
)


class WeightGather:
    def __init__(self, place, index, kind, width, source, target, send_sem, recv_sem):
        self.place, self.kind, self.width = place, kind, width
        self.orders = GATHER_ORDERS + (GATHER_ORDERS[index],)
        self.whole_dim = "ya" if index == 3 else "yb"
        self.source, self.target = source, target
        self.send_sem, self.recv_sem = send_sem, recv_sem

    def part(self, ref, chunk, fixed):
        rows, cols = span(self.kind, self.width, fixed)
        if self.kind == "tall":
            return ref.at[rows, pl.ds(chunk * 128, 128)]
        return ref.at[pl.ds(pl.multiple_of(chunk * 128 + rows.start, 16), rows.size), cols]

    def copy(self, chunk, step):
        place = self.place
        sems = (self.send_sem.at[chunk, step], self.recv_sem.at[chunk, step])
        if chunk == 5:
            return remote(place, self.whole_dim, self.part(self.source, chunk, ()), self.part(self.target, chunk, ()), *sems)
        order = self.orders[chunk]
        bits = [place.bit[dim] for dim in reversed(order)]
        if step == 0:
            return remote(place, "yb", self.part(self.source, chunk, bits), self.part(self.target, chunk, bits), *sems)
        bits = bits[: 5 - step]
        part = self.part(self.target, chunk, bits)
        return remote(place, order[step - 1], part, part, *sems)

    def begin(self, chunks):
        for chunk in chunks:
            self.copy(chunk, 0).start()

    def advance(self, step):
        for chunk in range(5):
            self.copy(chunk, step - 1).wait_recv()
            self.copy(chunk, step).start()

    def finish(self):
        for chunk in range(TYPES):
            self.copy(chunk, 4 if chunk < 5 else 0).wait_recv()

    def drain(self):
        for chunk in range(TYPES):
            for step in range(5 if chunk < 5 else 1):
                self.copy(chunk, step).wait_send()


SUM_ORDERS = (
    ("xa", "xb", "ya", "yb", "za", "zb"),
    ("xb", "xa", "yb", "ya", "zb", "za"),
    ("ya", "yb", "za", "zb", "xa", "xb"),
    ("yb", "ya", "zb", "za", "xb", "xa"),
    ("za", "zb", "xa", "xb", "ya", "yb"),
    ("zb", "za", "xb", "xa", "yb", "ya"),
)
SUM_ORDERS_X = SUM_ORDERS[:2] + (("xa", "xb", "za", "zb", "ya", "yb"),) + SUM_ORDERS[3:]
SUM_ORDERS_Z = SUM_ORDERS[:2] + (("zb", "za", "xb", "xa", "ya", "yb"),) + SUM_ORDERS[3:]
ALL_HALVES = pl.ds(0, 2)


class GradSum:
    def __init__(self, place, orders, width, held, landing, stage, out, sems):
        self.place, self.kind, self.width = place, "wide", width
        self.orders = orders
        self.held, self.landing, self.stage, self.out = held, landing, stage, out
        self.send_sem, self.recv_sem, self.ag_send, self.ag_recv, self.own_sem, self.stage_sem = sems

    def view(self, ref, half, chunk, fixed):
        rows, cols = span(self.kind, self.width, fixed)
        return ref.at[half, chunk, rows, cols]

    def moves(self, chunk, step):
        place = self.place
        order = self.orders[chunk]
        dim = order[step]
        regular = [d for d in order if d != "ya"]
        p, q, c = place.bit["ya"], place.bit["yb"], place.col
        y_at = [i for i, d in enumerate(order) if d[0] == "y"]
        a_first = order[y_at[0]] == "ya"
        own = [place.bit[d] for d in order[:step] if d != "ya"]
        flipped = [1 - bit for bit in own]
        if dim[0] != "y":
            bit = place.bit[dim]
            if step < y_at[0]:
                half_own = half_land = ALL_HALVES
            else:
                half_own = c
                half_land = c if a_first else 1 - c
            sent = [(half_own, own + [1 - bit])]
            lands = [(half_land, flipped + [1 - bit])]
            kept = [(half_own, own + [bit])]
            landed = [(half_land, flipped + [bit])]
            return dim, sent, lands, kept, landed
        if a_first and dim == "ya":
            sent = [(1 - p, own + [0]), (p, own + [1])]
            lands = [(1 - p, flipped + [0]), (p, flipped + [1])]
            kept = [(p, own + [0]), (1 - p, own + [1])]
            landed = [(p, flipped + [0]), (1 - p, flipped + [1])]
        elif a_first:
            send_half = (p + 1 - q) % 2
            sent = [(send_half, own + [1 - q])]
            lands = [(c, flipped + [1 - q])]
            kept = [(c, own + [q])]
            landed = [(1 - c, flipped + [q])]
        elif dim == "yb":
            sent = [(ALL_HALVES, own + [1 - q])]
            lands = [(ALL_HALVES, flipped + [1 - q])]
            kept = [(ALL_HALVES, own + [q])]
            landed = [(ALL_HALVES, flipped + [q])]
        else:
            sent = [(1 - c, own)]
            lands = [(1 - c, flipped)]
            kept = [(c, own)]
            landed = [(c, flipped)]
        return dim, sent, lands, kept, landed

    def sends(self, chunk, step):
        dim, sent, lands, _, _ = self.moves(chunk, step)
        return [
            remote(
                self.place,
                dim,
                self.view(self.held, *region),
                self.view(self.landing, *there),
                self.send_sem.at[chunk, step, index],
                self.recv_sem.at[chunk, step, index],
            )
            for index, (region, there) in enumerate(zip(
                [(h, chunk, b) for h, b in sent], [(h, chunk, b) for h, b in lands]
            ))
        ]

    def start(self, step):
        for chunk in range(TYPES):
            for copy in self.sends(chunk, step):
                copy.start()

    def staged(self, chunk, step, slot):
        _, _, _, kept, landed = self.moves(chunk, step)
        out = []
        for index, ((half, bits), (from_half, from_bits)) in enumerate(zip(kept, landed)):
            rows, cols = span(self.kind, self.width, bits)
            both = half is ALL_HALVES
            first = 32 * slot
            if not both and len(kept) == 1 and step > 0:
                index, first = slot, 0
            target = self.stage.at[
                chunk, pl.ds(0, 2) if both else index, pl.ds(first, rows.size), pl.ds(0, cols.size)
            ]
            source = self.view(self.landing, from_half, chunk, from_bits)
            copy = pltpu.make_async_copy(source, target, self.stage_sem.at[slot, chunk, len(out)])
            out.append((copy, half, rows, cols, index, first))
        return out

    def fetch(self, step, slot):
        for chunk in range(TYPES):
            for copy in self.sends(chunk, step):
                copy.wait_recv()
            for staged in self.staged(chunk, step, slot):
                staged[0].start()

    def add(self, step, slot):
        for chunk in range(TYPES):
            for copy, half, rows, cols, index, first in self.staged(chunk, step, slot):
                copy.wait()
                for h in range(2 if half is ALL_HALVES else 1):
                    here = h if half is ALL_HALVES else half
                    there = h if half is ALL_HALVES else index

                    def body(i, carry, here=here, there=there, rows=rows, cols=cols, first=first, chunk=chunk):
                        at = pl.multiple_of(i * 16, 16)
                        mine = (here, chunk, pl.ds(pl.multiple_of(rows.start + at, 16), 16), cols)
                        came = (chunk, there, pl.ds(pl.multiple_of(first + at, 16), 16), pl.ds(0, cols.size))
                        self.held[mine] = self.held[mine] + self.stage[came]
                        return carry

                    lax.fori_loop(0, rows.size // 16, body, 0)
            if step < 5:
                for copy in self.sends(chunk, step + 1):
                    copy.start()


    def spread(self, chunk, step):
        place = self.place
        order = self.orders[chunk]
        stages = []
        for d in reversed(order):
            if d[0] == "y":
                if "y2" not in stages:
                    stages.append("y2")
            else:
                stages.append(d)
        dim = stages[step]
        keep = [d for d in order if d != "ya"]
        done = set(stages[:step])
        bits = [place.bit[d] for d in keep if ("y2" if d == "yb" else d) not in done]
        rows, cols = span(self.kind, self.width, bits)
        target = self.out.at[chunk, rows, cols]
        source = self.held.at[place.col, chunk, rows, cols] if step == 0 else target
        return remote(place, dim, source, target, self.ag_send.at[chunk, step], self.ag_recv.at[chunk, step])

    def own(self, chunk):
        place = self.place
        bits = [place.bit[d] for d in self.orders[chunk] if d != "ya"]
        rows, cols = span(self.kind, self.width, bits)
        return pltpu.make_async_copy(
            self.held.at[place.col, chunk, rows, cols], self.out.at[chunk, rows, cols], self.own_sem.at[chunk]
        )

    def spread_start(self):
        for chunk in range(TYPES):
            self.spread(chunk, 0).start()
            self.own(chunk).start()

    def spread_next(self, step):
        for chunk in range(TYPES):
            if step == 1:
                self.own(chunk).wait()
            self.spread(chunk, step - 1).wait_recv()
            self.spread(chunk, step).start()

    def finish(self):
        for chunk in range(TYPES):
            self.spread(chunk, 4).wait_recv()

    def release(self):
        for chunk in range(TYPES):
            for step in range(6):
                for copy in self.sends(chunk, step):
                    copy.wait_send()
            self.spread(chunk, 0).wait_send()

    def drain(self):
        for chunk in range(TYPES):
            for step in range(1, 5):
                self.spread(chunk, step).wait_send()


HEAD_DIM = 96
EPS = 1e-05
ROPE_BASE = 100000.0
NEG = -1e30
SCALE = 1.0 / math.sqrt(HEAD_DIM)
ANYWHERE = pl.BlockSpec(memory_space=pl.ANY)


def matmul(left, right):
    return jnp.dot(left, right, preferred_element_type=F32)


def inner_left(left, right):
    return lax.dot_general(left, right, (((0,), (0,)), ((), ())), preferred_element_type=F32)


def inner_right(left, right):
    return lax.dot_general(left, right, (((1,), (1,)), ((), ())), preferred_element_type=F32)


def rotary_tables():
    rates = ROPE_BASE ** (-2.0 * np.arange(HEAD_DIM // 2) / HEAD_DIM)
    angle = np.arange(1024)[:, None] * rates[None, :]
    cosine, sine = np.cos(angle), np.sin(angle)
    return (
        np.concatenate([cosine, cosine], axis=1).astype(np.float32),
        np.concatenate([-sine, sine], axis=1).astype(np.float32),
    )


def swap_halves(value):
    half = HEAD_DIM // 2
    return jnp.concatenate([value[:, half:], value[:, :half]], axis=1)


def head_of(value, head):
    return value[:, head * HEAD_DIM : (head + 1) * HEAD_DIM]


def pad_head(value):
    return jnp.concatenate([value, jnp.zeros((value.shape[0], 128 - HEAD_DIM), value.dtype)], axis=1)


def aligned(start, size, step):
    return pl.ds(pl.multiple_of(start, step), size)


def masked_scores(query, keys, start):
    raw = inner_right(query, keys) * SCALE
    place = start + lax.broadcasted_iota(jnp.int32, raw.shape, 0)
    return jnp.where(lax.broadcasted_iota(jnp.int32, raw.shape, 1) <= place, raw, NEG)


FORWARD_KEEPS = (
    ("gains", (8, 1536), F32),
    ("x", (512, 1536), BF16),
    ("s1", (1024, 1536), BF16),
    ("og", (512, 1536), BF16),
    ("qh", (8, 512, 128), BF16),
    ("kh", (4, 1024, 128), BF16),
    ("vh", (4, 1024, 128), BF16),
    ("attended", (512, 768), BF16),
    ("middle", (256, 1536), F32),
    ("s2", (512, 1536), BF16),
    ("hidden", (512, 2048), BF16),
    ("slope", (512, 2048), BF16),
    ("active", (512, 2048), BF16),
    ("block", (256, 1536), BF16),
)
WEIGHTS = (("wide", 2304), ("wide", 2048), ("wide", 2048), ("tall", 2048))


def weight_shape(kind, width):
    return (width, 768) if kind == "tall" else (768, width)


def forward(w_parts, w_gate, w_up, w_down, hidden_in, out_grad, gains, cosine, sine, ident):
    keeps = len(FORWARD_KEEPS)

    def kernel(*refs):
        att_parts, sources, (hid, ogr, gain, cos_t, sin_t) = refs[:4], refs[4:7], refs[7:12]
        others, kept_out = refs[12:16], refs[16 : 16 + keeps]
        refs = refs[16 + keeps :]
        v = {name: ref for (name, _, _), ref in zip(FORWARD_KEEPS, refs[:keeps])}
        (att_v, gate_v, up_v, down_v, cos_v, sin_v, oh, outgo, came1, came2, send_sem, recv_sem, small_send,
         small_recv, local_sem, load_sem, keep_sem) = refs[keeps:]
        place = Place()
        row, col = place.row, place.col
        own_cols = aligned(col * 768, 768, 128)
        their_cols = aligned((1 - col) * 768, 768, 128)
        own_rows = aligned(row * 256, 256, 256)
        their_rows = aligned((1 - row) * 256, 256, 256)
        mine = aligned(col * 256, 256, 256)
        theirs = aligned((1 - col) * 256, 256, 256)

        def small(index, dim, src, dst):
            return remote(place, dim, src, dst, small_send.at[index], small_recv.at[index])

        def local(index, src, dst):
            return pltpu.make_async_copy(src, dst, local_sem.at[index])

        keep_order = [name for name, _, _ in FORWARD_KEEPS]

        def keep(name):
            index = keep_order.index(name)
            return pltpu.make_async_copy(v[name], kept_out[index], keep_sem.at[index])

        att_loads = [
            local(5 + k, part, att_v.at[own_cols, pl.ds(at, part.shape[1])])
            for k, (part, at) in enumerate(zip(att_parts, (0, 768, 1152, 1536)))
        ]
        x_load = local(0, hid, v["x"].at[:, own_cols])
        gain_load = local(1, gain, v["gains"].at[:, own_cols])
        og_load = local(2, ogr.at[mine], v["og"].at[own_rows, own_cols])
        cos_load = local(3, cos_t, cos_v)
        sin_load = local(4, sin_t, sin_v)
        for copy in att_loads + [x_load, gain_load, og_load, cos_load, sin_load]:
            copy.start()
        greet(place, ALL_DIMS + ("row",))
        x_moves = [
            small(k, "ya", hid.at[pl.ds(k * 256, 256)], v["x"].at[pl.ds(k * 256, 256), own_cols]) for k in range(2)
        ]
        gain_move = small(2, "ya", gain, v["gains"].at[:, own_cols])
        og_move = small(3, "ya", ogr.at[theirs], v["og"].at[own_rows, own_cols])
        gain_move.start()
        for copy in x_moves:
            copy.start()
        jobs = [
            WeightGather(place, index, kind, width, source, other, send_sem.at[index], recv_sem.at[index])
            for index, ((kind, width), source, other) in enumerate(
                zip(WEIGHTS, (att_v.at[own_cols],) + tuple(sources), others)
            )
        ]
        att, gate_j, up_j, down_j = jobs
        mlp = (gate_j, up_j, down_j)
        for copy in att_loads:
            copy.wait()
        att.begin(range(5))
        for job in mlp:
            job.begin(range(5))
        att.begin((5,))
        whole = (att_v, gate_v, up_v, down_v)
        own_loads, other_loads = [None], []
        for index, ((kind, _), other, target) in enumerate(zip(WEIGHTS, others, whole)):
            tall = kind == "tall"
            if index > 0:
                own_loads.append(
                    pltpu.make_async_copy(
                        sources[index - 1], target.at[:, own_cols] if tall else target.at[own_cols], load_sem.at[0, index]
                    )
                )
                own_loads[index].start()
            other_loads.append(
                pltpu.make_async_copy(
                    other, target.at[:, their_cols] if tall else target.at[their_cols], load_sem.at[1, index]
                )
            )

        def norm_into(read, gain_row, target, start):
            def block(i, carry):
                value = read(i)
                factor = lax.rsqrt(jnp.mean(value * value, axis=1, keepdims=True) + EPS)
                target[aligned(start + i * 32, 32, 32)] = (
                    value * factor * v["gains"][gain_row : gain_row + 1, :]
                ).astype(BF16)
                return carry

            lax.fori_loop(0, 8, block, 0)

        x_load.wait()
        gain_load.wait()
        gain_move.wait_recv()
        att.advance(1)
        s1_moves = []
        for part in range(2):
            x_moves[part].wait_recv()
            start = row * 512 + part * 256
            norm_into(lambda i: v["x"][aligned(part * 256 + i * 32, 32, 32)].astype(F32), 0, v["s1"], start)
            rows = aligned(start, 256, 256)
            s1_moves.append(small(4 + part, "row", v["s1"].at[rows], v["s1"].at[rows]))
            s1_moves[part].start()
            if part == 0:
                att.advance(2)
                for job in mlp:
                    job.advance(1)
                att.advance(3)
        og_move.start()
        att.advance(4)
        for job in mlp:
            job.advance(2)
        for job in mlp:
            job.begin((5,))
        keep("x").start()
        keep("gains").start()
        cos_load.wait()
        sin_load.wait()
        for copy in s1_moves:
            copy.wait_recv()
        keep("s1").start()
        att.finish()
        other_loads[0].start()
        for job in mlp:
            job.advance(3)
        other_loads[0].wait()

        def turned(value, rows):
            return value * cos_v[rows] + swap_halves(value) * sin_v[rows]

        for part in range(4):
            rows = slice(part * 256, part * 256 + 256)
            value = matmul(v["s1"][rows], att_v[:, 768:1536])
            for head in range(4):
                v["kh"][head, rows] = pad_head(turned(head_of(value, head), rows).astype(BF16))
                v["vh"][head, rows] = pad_head(head_of(value, 4 + head).astype(BF16))
        for part in range(2):
            places = aligned(part * 512 + col * 256, 256, 256)
            rows = slice(part * 256, part * 256 + 256)
            value = matmul(v["s1"][places], att_v[:, 0:768])
            for head in range(8):
                v["qh"][head, rows] = pad_head(turned(head_of(value, head), places).astype(BF16))
        for name in ("qh", "kh", "vh"):
            keep(name).start()

        def heads(h, carry):
            for pair in range(2):
                for at, reach in ((0, 512), (256, 1024)):
                    scores = masked_scores(
                        v["qh"][h * 2 + pair, at : at + 256], v["kh"][h, 0:reach], at * 2 + col * 256
                    )
                    powers = jnp.exp(scores - jnp.max(scores, axis=1, keepdims=True))
                    total = jnp.sum(powers, axis=1, keepdims=True)
                    shares = (powers * (1.0 / total)).astype(BF16)
                    oh[h * 2 + pair, at : at + 256] = matmul(shares, v["vh"][h, 0:reach]).astype(BF16)
            return carry

        lax.fori_loop(0, 2, heads, 0)
        for job in mlp:
            job.advance(4)
        lax.fori_loop(2, 4, heads, 0)
        v["attended"][...] = jnp.concatenate([oh[j][:, 0:HEAD_DIM] for j in range(8)], axis=1)
        keep("attended").start()

        def summed(index, read, weight, came, done):
            def half(rows, put):
                left = read(rows)
                for h in range(3):
                    put(h, matmul(left, weight(h)))

            def put_out(h, value):
                outgo[:, h * 512 : h * 512 + 512] = value

            half(their_rows, put_out)
            move = small(index, "row", outgo, came)
            move.start()
            half(own_rows, done)
            move.wait_recv()
            return move

        def out_weight(h):
            if h == 0:
                return att_v[0:768, 1536 : 1536 + 512]
            if h == 2:
                return att_v[768:1536, 1536 + 256 : 2304]
            return jnp.concatenate([att_v[0:768, 2048:2304], att_v[768:1536, 1536:1792]], axis=1)

        def add_middle(h, value):
            at = h * 512
            v["middle"][:, at : at + 512] = v["x"][mine, at : at + 512].astype(F32) + value

        out_move = summed(6, lambda rows: v["attended"][rows], out_weight, came1, add_middle)
        v["middle"][...] = v["middle"][...] + came1[...]
        keep("middle").start()
        norm_into(lambda i: v["middle"][aligned(i * 32, 32, 32)], 1, v["s2"], row * 256)
        s2_move = small(7, "row", v["s2"].at[own_rows], v["s2"].at[own_rows])
        s2_move.start()
        og_load.wait()
        og_move.wait_recv()
        og_swap = small(8, "row", v["og"].at[own_rows], v["og"].at[own_rows])
        og_swap.start()
        for index, job in ((1, gate_j), (2, up_j)):
            own_loads[index].wait()
            job.finish()
            other_loads[index].start()
        s2_move.wait_recv()
        keep("s2").start()
        og_swap.wait_recv()
        keep("og").start()
        other_loads[1].wait()
        other_loads[2].wait()

        def units(n, carry):
            cols = aligned(n * 256, 256, 256)
            gate = matmul(v["s2"][...], gate_v[:, cols])
            upper = matmul(v["s2"][...], up_v[:, cols])
            logistic = 1.0 / (1.0 + jnp.exp(-gate))
            active = gate * logistic
            v["hidden"][:, cols] = (active * upper).astype(BF16)
            v["slope"][:, cols] = (upper * logistic * (1.0 + gate * (1.0 - logistic))).astype(BF16)
            v["active"][:, cols] = active.astype(BF16)
            return carry

        lax.fori_loop(0, 8, units, 0)
        for name in ("hidden", "slope", "active"):
            keep(name).start()
        own_loads[3].wait()
        down_j.finish()
        other_loads[3].start()
        out_move.wait_send()
        other_loads[3].wait()

        def add_out(h, value):
            at = h * 512
            came1[:, at : at + 512] = v["middle"][:, at : at + 512] + value

        down_move = summed(
            9, lambda rows: v["hidden"][rows], lambda h: down_v[:, h * 512 : h * 512 + 512], came2, add_out
        )
        v["block"][...] = (came1[...] + came2[...]).astype(BF16)
        keep("block").start()
        for job in jobs:
            job.drain()
        for copy in x_moves + s1_moves + [gain_move, og_move, s2_move, og_swap, down_move]:
            copy.wait_send()
        for name in keep_order:
            keep(name).wait()

    outs = [jax.ShapeDtypeStruct(weight_shape(*w), BF16) for w in WEIGHTS]
    outs += [jax.ShapeDtypeStruct(shape, kind) for _, shape, kind in FORWARD_KEEPS]
    return pl.pallas_call(
        kernel,
        out_shape=outs,
        in_specs=[ANYWHERE] * 12,
        out_specs=[ANYWHERE] * (4 + keeps),
        scratch_shapes=[pltpu.VMEM(shape, kind) for _, shape, kind in FORWARD_KEEPS]
        + [
            pltpu.VMEM((1536, 2304), BF16),
            pltpu.VMEM((1536, 2048), BF16),
            pltpu.VMEM((1536, 2048), BF16),
            pltpu.VMEM((2048, 1536), BF16),
            pltpu.VMEM((1024, HEAD_DIM), F32),
            pltpu.VMEM((1024, HEAD_DIM), F32),
            pltpu.VMEM((8, 512, 128), BF16),
            pltpu.VMEM((256, 1536), F32),
            pltpu.VMEM((256, 1536), F32),
            pltpu.VMEM((256, 1536), F32),
            pltpu.SemaphoreType.DMA((4, TYPES, 5)),
            pltpu.SemaphoreType.DMA((4, TYPES, 5)),
            pltpu.SemaphoreType.DMA((10,)),
            pltpu.SemaphoreType.DMA((10,)),
            pltpu.SemaphoreType.DMA((9,)),
            pltpu.SemaphoreType.DMA((2, 4)),
            pltpu.SemaphoreType.DMA((keeps,)),
        ],
        compiler_params=pltpu.CompilerParams(
            collective_id=ident, has_side_effects=True, vmem_limit_bytes=63 << 20
        ),
        name="forward",
    )(*w_parts, w_gate, w_up, w_down, hidden_in, out_grad, gains, cosine, sine)


GROUP_WIDTHS = (2048, 2048, 2048, 2560)
SERVED = {
    "gated": "",
    "up": "",
    "e0": "D",
    "e1": "d",
    "e2": "",
    "e3": "",
    "e4": "",
    "expanded": "G",
    "normed": "g",
    "attended": "D",
    "head0": "dU",
    "head1": "uG",
    "head2": "gD",
    "heads": "dU",
    "packed": "uG",
    "projected": "gD",
    "started": "dUuGgD",
    "input": "dUuG",
    "done": "gDdUu",
    "rest": "AadgunAadgunAadgunAadgunmAanAandguanguaa"
    "aa",
}


def backward(w_parts, mlp_weights, other_weights, kept, cosine, sine, ident):
    keeps = len(FORWARD_KEEPS)
    groups = len(GROUP_WIDTHS)
    names = [name for name, _, _ in FORWARD_KEEPS]

    def kernel(*refs):
        att_parts, (w_gate, w_up, w_down), (o_att, o_gate, o_up, o_down) = refs[0:4], refs[4:7], refs[7:11]
        hbm = dict(zip(names, refs[11 : 11 + keeps]))
        cos_t, sin_t = refs[11 + keeps : 13 + keeps]
        refs = refs[13 + keeps :]
        sums, landing, (bo_out, ig_out, gain_out) = refs[:groups], refs[groups : 2 * groups], refs[2 * groups : 2 * groups + 3]
        (held0, held1, held2, acts, stage, pool, og, qh, kh, vh, doh, attended, dk, dv, part_kv, kv_in,
         dqkv, cos_v, sin_v, outgo, mine_v, came1, came2, middle, x_v, gains, gain_sum, gain_came, ig_v, bo_v,
         rs_send, rs_recv, ag_send, ag_recv, own_sem, stage_sem, load_sem, pool_sem, small_send, small_recv,
        ) = refs[2 * groups + 3 :]
        place = Place()
        row, col = place.row, place.col
        own_cols = aligned(col * 768, 768, 128)
        their_cols = aligned((1 - col) * 768, 768, 128)
        own_rows = aligned(row * 256, 256, 256)
        their_rows = aligned((1 - row) * 256, 256, 256)
        mine = aligned(col * 256, 256, 256)
        theirs = aligned((1 - col) * 256, 256, 256)

        def small(index, dim, src, dst):
            return remote(place, dim, src, dst, small_send.at[index], small_recv.at[index])

        held = (held0, held1, held2, acts)
        flat = acts.reshape(2 * TYPES * 128, 2560)
        slope, active, units = (flat.at[pl.ds(k * 512, 512), pl.ds(0, 2048)] for k in range(3))
        orders = (SUM_ORDERS,) * 4
        down, gate, up, att = [
            GradSum(
                place, orders[g], width, held[g], landing[g], stage, sums[g],
                (rs_send.at[g], rs_recv.at[g], ag_send.at[g], ag_recv.at[g], own_sem.at[g], stage_sem),
            )
            for g, width in enumerate(GROUP_WIDTHS)
        ]
        served, fetched = {}, {}

        def serve(point):
            for letter in SERVED[point]:
                name = letter.lower()
                step = served.get(name, 0)
                job = {"d": down, "g": gate, "u": up, "a": att}.get(name)
                if job is not None and step < 6 and name not in fetched:
                    free = {0, 1} - set(fetched.values())
                    assert 0 in free if step == 0 else free
                    assert step > 0 or len(free) == 2
                    fetched[name] = min(free)
                    job.fetch(step, fetched[name])
                if letter != name:
                    continue
                if name == "m":
                    bo_move.start()
                    ig_move.start()
                    continue
                served[name] = step + 1
                if job is None:
                    gain_step(step + 1)
                elif step < 6:
                    job.add(step, fetched.pop(name))
                    if step == 5:
                        job.spread_start()
                elif step < 10:
                    job.spread_next(step - 5)
                else:
                    job.finish()

        loads = {}

        def load(name, source, target):
            copy = pltpu.make_async_copy(source, target, load_sem.at[len(loads)])
            copy.start()
            loads[name] = copy

        def down_tile(n):
            at = pl.ds(pl.multiple_of(1024 + (n % 2) * 256, 256), 256)
            rows = pl.ds(pl.multiple_of(n * 256, 256), 256)
            return [
                pltpu.make_async_copy(w_down.at[rows], pool.at[at, own_cols], pool_sem.at[n % 2, 0]),
                pltpu.make_async_copy(o_down.at[rows], pool.at[at, their_cols], pool_sem.at[n % 2, 1]),
            ]

        def expand_tile(n):
            sources = (w_gate, w_up) if n < 3 else (o_gate, o_up)
            rows = pl.ds((n % 3) * 256, 256)
            slot = n % 2
            return [
                pltpu.make_async_copy(
                    source.at[rows], pool.at[pl.ds((slot * 2 + k) * 256, 256)], pool_sem.at[2 + slot, k]
                )
                for k, source in enumerate(sources)
            ]

        load("og", hbm["og"], og)
        load("hidden", hbm["hidden"], units)
        for copy in down_tile(0):
            copy.start()
        load("slope", hbm["slope"], slope)
        load("active", hbm["active"], active)
        for n in range(2):
            for copy in expand_tile(n):
                copy.start()
        load("middle", hbm["middle"], middle)
        load("gains", hbm["gains"], gains)
        load("qh", hbm["qh"], qh)
        load("kh", hbm["kh"], kh)
        load("vh", hbm["vh"], vh)
        load("attended", hbm["attended"], attended)
        load("cos", cos_t, cos_v)
        load("sin", sin_t, sin_v)
        load("x", hbm["x"].at[mine], x_v)
        load("block", hbm["block"], bo_v)
        greet(place, ALL_DIMS + ("y2", "row"))

        def weight_grad(left, right, target, at, blocks, cols):
            def block(i, carry):
                half, pair = i // 3, i % 3
                lhs = left[:, aligned(i * 256, 256, 256)]
                for n in range(cols // 512):
                    value = inner_left(lhs, right[:, n * 512 : n * 512 + 512]).astype(BF16)
                    for k in range(2):
                        target[half, pair * 2 + k, :, at + n * 512 : at + n * 512 + 512] = value[k * 128 : k * 128 + 128]
                return carry

            lax.fori_loop(0, blocks, block, 0)

        loads["og"].wait()
        loads["hidden"].wait()
        weight_grad(og, units, held0, 0, 6, 2048)
        down.start(0)
        load("s2", hbm["s2"], units.at[:, pl.ds(0, 1536)])
        loads["slope"].wait()
        loads["active"].wait()

        def hidden_tile(n, carry):
            @pl.when(n < 7)
            def _():
                for copy in down_tile(n + 1):
                    copy.start()

            for copy in down_tile(n):
                copy.wait()
            weight = pool[pl.ds(pl.multiple_of(1024 + (n % 2) * 256, 256), 256), 0:1536]
            grad = inner_right(og[...], weight)
            cols = aligned(n * 256, 256, 256)
            slope[:, cols] = (grad * slope[:, cols].astype(F32)).astype(BF16)
            active[:, cols] = (grad * active[:, cols].astype(F32)).astype(BF16)
            return carry

        lax.fori_loop(0, 8, hidden_tile, 0)
        loads["s2"].wait()
        weight_grad(units, slope, held1, 0, 6, 2048)
        gate.start(0)
        serve("gated")
        weight_grad(units, active, held2, 0, 6, 2048)
        up.start(0)
        serve("up")
        loads["block"].wait()
        bo_move = small(6, "ya", bo_v.at[:, their_cols], bo_out.at[mine])
        bo_own = pltpu.make_async_copy(bo_v.at[:, own_cols], bo_out.at[mine], pool_sem.at[4, 0])
        bo_own.start()

        for n in range(6):
            for copy in expand_tile(n):
                copy.wait()
            slot = (n % 2) * 512
            cols = aligned((col if n < 3 else 1 - col) * 768 + (n % 3) * 256, 256, 256)
            for rows, target in ((their_rows, outgo), (own_rows, mine_v)):
                target[:, cols] = inner_right(slope[rows], pool[slot : slot + 256, :]) + inner_right(
                    active[rows], pool[slot + 256 : slot + 512, :]
                )
            if n + 2 < 6:
                for copy in expand_tile(n + 2):
                    copy.start()
            if n < 5:
                serve("e%d" % n)
        mlp_move = small(0, "row", outgo, came1)
        mlp_move.start()
        load("out_own", att_parts[3], pool.at[pl.ds(0, 768), own_cols])
        load("out_other", o_att.at[:, pl.ds(1536, 768)], pool.at[pl.ds(0, 768), their_cols])
        serve("expanded")
        loads["middle"].wait()
        loads["gains"].wait()
        mlp_move.wait_recv()

        gain_sum[0] = jnp.zeros((8, 1536), F32)

        def norm_back(value_of, grad_came, gain_row, finish):

            def block(i, carry):
                rows = aligned(i * 32, 32, 32)
                value = value_of(rows)
                grad = mine_v[rows] + grad_came[rows]
                factor = lax.rsqrt(jnp.mean(value * value, axis=1, keepdims=True) + EPS)
                normed = value * factor
                gain_sum[0, gain_row : gain_row + 1, :] += jnp.sum(grad * normed, axis=0, keepdims=True)
                scaled = grad * gains[gain_row : gain_row + 1, :]
                back = factor * (scaled - normed * jnp.mean(scaled * normed, axis=1, keepdims=True))
                finish(i, rows, back)
                return carry

            lax.fori_loop(0, 8, block, 0)

        def put_middle(i, rows, back):
            at = aligned(row * 256 + i * 32, 32, 32)
            total = og[at].astype(F32) + back
            middle[rows] = total
            og[at] = total.astype(BF16)

        norm_back(lambda rows: middle[rows], came1, 1, put_middle)
        gm_move = small(1, "row", og.at[own_rows], og.at[own_rows])
        gm_move.start()
        loads["out_own"].wait()
        loads["out_other"].wait()
        serve("normed")
        gm_move.wait_recv()

        for part in range(2):
            value = inner_right(og[...], pool[part * 384 : part * 384 + 384, 0:1536]).astype(BF16)
            for head in range(4):
                doh[part * 4 + head] = pad_head(value[:, head * HEAD_DIM : (head + 1) * HEAD_DIM])
        load("s1", hbm["s1"], pool.at[pl.ds(0, 1024), pl.ds(0, 1536)])
        serve("attended")
        for name in ("qh", "kh", "vh", "cos", "sin"):
            loads[name].wait()

        def turned_back(value, places):
            return value * cos_v[places] - swap_halves(value) * sin_v[places]

        def heads(h, carry):
            dk[...] = jnp.zeros((1024, 128), F32)
            dv[...] = jnp.zeros((1024, 128), F32)
            for pair in range(2):
                for at, reach in ((0, 512), (256, 1024)):
                    rows = slice(at, at + 256)
                    query, grad = qh[h * 2 + pair, rows], doh[h * 2 + pair, rows]
                    keys, values = kh[h, 0:reach], vh[h, 0:reach]
                    scores = masked_scores(query, keys, at * 2 + col * 256)
                    powers = jnp.exp(scores - jnp.max(scores, axis=1, keepdims=True))
                    shares = powers * (1.0 / jnp.sum(powers, axis=1, keepdims=True))
                    grad_shares = inner_right(grad, values)
                    center = jnp.sum(grad_shares * shares, axis=1, keepdims=True)
                    grad_raw = (shares * (grad_shares - center) * SCALE).astype(BF16)
                    dk[0:reach] += inner_left(grad_raw, query)
                    dv[0:reach] += inner_left(shares.astype(BF16), grad)
                    value = turned_back(matmul(grad_raw, keys)[:, 0:HEAD_DIM], aligned(at * 2 + col * 256, 256, 256))
                    qh[h * 2 + pair, rows] = pad_head(value.astype(BF16))
            for part in range(4):
                rows = slice(part * 256, part * 256 + 256)
                kh[h, rows] = pad_head(turned_back(dk[rows, 0:HEAD_DIM], rows).astype(BF16))
            vh[h] = dv[...].astype(BF16)
            return carry

        for h in range(4):
            lax.fori_loop(h, h + 1, heads, 0)
            if h < 3:
                serve("head%d" % h)
        serve("heads")
        for part in range(4):
            rows = slice(part * 256, part * 256 + 256)
            part_kv[rows] = jnp.concatenate(
                [kh[h, rows][:, 0:HEAD_DIM] for h in range(4)] + [vh[h, rows][:, 0:HEAD_DIM] for h in range(4)], axis=1
            )
        kv_moves = [
            small(2 + part, "ya", part_kv.at[aligned(part * 512 + (1 - col) * 256, 256, 256)],
                  kv_in.at[pl.ds(part * 256, 256)])
            for part in range(2)
        ]
        for copy in kv_moves:
            copy.start()
        dqkv[:, 0:768] = jnp.concatenate([qh[j][:, 0:HEAD_DIM] for j in range(8)], axis=1)
        serve("packed")
        loads["s1"].wait()
        loads["attended"].wait()

        def projection_grads(i, carry):
            half, pair = i // 3, i % 3
            features = aligned(i * 256, 256, 256)
            parts = [pool[aligned(part * 512 + col * 256, 256, 256), features] for part in range(2)]
            whole = pool[0:1024, features]

            def put(at, value):
                value = value.astype(BF16)
                for k in range(2):
                    acts[half, pair * 2 + k, :, at : at + 384] = value[k * 128 : k * 128 + 128]

            for n in range(2):
                cols = slice(n * 384, n * 384 + 384)
                put(n * 384, inner_left(parts[0], dqkv[0:256, cols]) + inner_left(parts[1], dqkv[256:512, cols]))
                put(768 + n * 384, inner_left(whole, part_kv[:, cols]))
            return carry

        lax.fori_loop(0, 6, projection_grads, 0)
        serve("projected")
        load("qkv_other", o_att.at[:, pl.ds(0, 1536)], pool.at[their_cols, pl.ds(0, 1536)])
        for k, at in enumerate((0, 768, 1152)):
            load(k, att_parts[k], pool.at[own_cols, pl.ds(at, att_parts[k].shape[1])])

        def out_grads(i, carry):
            lhs = attended[:, aligned(i * 256, 256, 256)]
            for half in range(2):
                value = inner_left(lhs, og[:, half * 768 : half * 768 + 768]).astype(BF16)
                for k in range(2):
                    acts[half, i * 2 + k, :, 1536:2304] = value[k * 128 : k * 128 + 128]
            return carry

        lax.fori_loop(0, 3, out_grads, 0)
        acts[:, :, :, 2304:2560] = jnp.zeros((2, TYPES, 128, 256), BF16)
        att.start(0)

        serve("started")
        for copy in kv_moves:
            copy.wait_recv()
        for part in range(2):
            rows = slice(part * 256, part * 256 + 256)
            own = part_kv[aligned(part * 512 + col * 256, 256, 256)].astype(F32)
            dqkv[rows, 768:1536] = (own + kv_in[rows].astype(F32)).astype(BF16)
        loads["qkv_other"].wait()
        for k in range(3):
            loads[k].wait()
        mlp_move.wait_send()
        for n in range(3):
            cols = slice(n * 512, n * 512 + 512)
            for rows, target in ((their_rows, outgo), (own_rows, mine_v)):
                target[:, cols] = inner_right(dqkv[rows], pool[cols, 0:1536])
        att_move = small(4, "row", outgo, came2)
        att_move.start()
        serve("input")
        loads["x"].wait()
        att_move.wait_recv()

        def put_input(i, rows, back):
            ig_v[rows] = (middle[rows] + back).astype(BF16)

        norm_back(lambda rows: x_v[rows].astype(F32), came2, 0, put_input)
        ig_move = small(5, "ya", ig_v.at[:, their_cols], ig_out.at[mine])
        ig_own = pltpu.make_async_copy(ig_v.at[:, own_cols], ig_out.at[mine], pool_sem.at[4, 1])
        ig_own.start()

        gain_dims = ("row",) + ALL_DIMS
        gain_moves = [small(7 + k, dim, gain_sum.at[k], gain_came.at[k]) for k, dim in enumerate(gain_dims)]

        def gain_step(k):
            if k > 0:
                gain_moves[k - 1].wait_recv()
                gain_sum[k] = gain_sum[k - 1] + gain_came[k - 1]
            if k < len(gain_dims):
                gain_moves[k].start()

        gain_step(0)

        serve("done")
        serve("rest")
        gain_own = pltpu.make_async_copy(gain_sum.at[7, :, own_cols], gain_out, pool_sem.at[4, 0])
        bo_own.wait()
        gain_own.start()
        ig_own.wait()
        gain_own.wait()
        for copy in [gm_move, att_move] + kv_moves + gain_moves:
            copy.wait_send()
        ig_move.wait()
        bo_move.wait()
        for job in (down, gate, up, att):
            job.release()
        for job in (down, gate, up, att):
            job.drain()

    chunk_shapes = [(TYPES, 128, width) for width in GROUP_WIDTHS]
    outs = [jax.ShapeDtypeStruct(shape, BF16) for shape in chunk_shapes]
    outs += [jax.ShapeDtypeStruct((2,) + shape, BF16) for shape in chunk_shapes]
    outs += [jax.ShapeDtypeStruct((512, 768), BF16)] * 2 + [jax.ShapeDtypeStruct((8, 768), F32)]
    dma = pltpu.SemaphoreType.DMA
    return pl.pallas_call(
        kernel,
        out_shape=outs,
        in_specs=[ANYWHERE] * (13 + keeps),
        out_specs=[ANYWHERE] * len(outs),
        scratch_shapes=[
            pltpu.VMEM((2, TYPES, 128, 2048), BF16),
            pltpu.VMEM((2, TYPES, 128, 2048), BF16),
            pltpu.VMEM((2, TYPES, 128, 2048), BF16),
            pltpu.VMEM((2, TYPES, 128, 2560), BF16),
            pltpu.VMEM((TYPES, 2, 64, 2560), BF16),
            pltpu.VMEM((1536, 2048), BF16),
            pltpu.VMEM((512, 1536), BF16),
            pltpu.VMEM((8, 512, 128), BF16),
            pltpu.VMEM((4, 1024, 128), BF16),
            pltpu.VMEM((4, 1024, 128), BF16),
            pltpu.VMEM((8, 512, 128), BF16),
            pltpu.VMEM((512, 768), BF16),
            pltpu.VMEM((1024, 128), F32),
            pltpu.VMEM((1024, 128), F32),
            pltpu.VMEM((1024, 768), BF16),
            pltpu.VMEM((512, 768), BF16),
            pltpu.VMEM((512, 1536), BF16),
            pltpu.VMEM((1024, HEAD_DIM), F32),
            pltpu.VMEM((1024, HEAD_DIM), F32),
            pltpu.VMEM((256, 1536), F32),
            pltpu.VMEM((256, 1536), F32),
            pltpu.VMEM((256, 1536), F32),
            pltpu.VMEM((256, 1536), F32),
            pltpu.VMEM((256, 1536), F32),
            pltpu.VMEM((256, 1536), BF16),
            pltpu.VMEM((8, 1536), F32),
            pltpu.VMEM((8, 8, 1536), F32),
            pltpu.VMEM((7, 8, 1536), F32),
            pltpu.VMEM((256, 1536), BF16),
            pltpu.VMEM((256, 1536), BF16),
            dma((groups, TYPES, 6, 2)),
            dma((groups, TYPES, 6, 2)),
            dma((groups, TYPES, 5)),
            dma((groups, TYPES, 5)),
            dma((groups, TYPES)),
            dma((2, TYPES, 2)),
            dma((24,)),
            dma((5, 2)),
            dma((14,)),
            dma((14,)),
        ],
        compiler_params=pltpu.CompilerParams(
            collective_id=ident, has_side_effects=True, vmem_limit_bytes=63 << 20
        ),
        name="backward",
    )(*w_parts, *mlp_weights, *other_weights, *kept, cosine, sine)


def widen(sum_down, sum_gate, sum_up, sum_att):
    def kernel(down, gate, up, att, query_out, key_out, value_out, out_out, gate_out, up_out, down_out):
        at = 0
        for target in (query_out, key_out, value_out, out_out):
            width = target.shape[1]
            target[...] = att[0, :, at : at + width].astype(F32)
            at += width
        gate_out[...] = gate[0].astype(F32)
        up_out[...] = up[0].astype(F32)
        down_out[...] = down[0].astype(F32).T

    widths = (768, 384, 384, 768, 2048, 2048)
    return pl.pallas_call(
        kernel,
        grid=(TYPES,),
        out_shape=[jax.ShapeDtypeStruct((768, width), F32) for width in widths]
        + [jax.ShapeDtypeStruct((2048, 768), F32)],
        in_specs=[pl.BlockSpec((1, 128, width), lambda i: (i, 0, 0)) for width in GROUP_WIDTHS],
        out_specs=[pl.BlockSpec((128, width), lambda i: (i, 0)) for width in widths]
        + [pl.BlockSpec((2048, 128), lambda i: (0, i))],
        compiler_params=pltpu.CompilerParams(vmem_limit_bytes=40 << 20),
        name="widen",
    )(sum_down, sum_gate, sum_up, sum_att)


def per_device(
    hidden_in, gain_attn, w_query, w_key, w_value, w_out, gain_mlp, w_gate, w_up, w_down, out_grad
):
    w_parts = (w_query, w_key, w_value, w_out)
    gains = jnp.concatenate([gain_attn[None], gain_mlp[None], jnp.zeros((6, 768), F32)], axis=0)
    cosine, sine = (jnp.asarray(table) for table in rotary_tables())
    done = forward(w_parts, w_gate, w_up, w_down, hidden_in, out_grad, gains, cosine, sine, 1)
    back = backward(w_parts, (w_gate, w_up, w_down), done[:4], done[4:], cosine, sine, 2)
    block_out, in_grad, gain_grads = back[8:]
    sums = widen(*back[:4])
    return (block_out, in_grad, gain_grads[0]) + tuple(sums[:4]) + (gain_grads[1],) + tuple(sums[4:])


def solution(mesh):
    tokens, weight_in, weight_out, gain = P(("dp", "row"), "col"), P("col", "row"), P("row", "col"), P("col")
    return jax.shard_map(
        per_device,
        mesh=mesh,
        in_specs=(
            tokens, gain, weight_in, weight_in, weight_in, weight_out, gain, weight_in, weight_in, weight_out, tokens,
        ),
        out_specs=(
            tokens, tokens, gain, weight_in, weight_in, weight_in, weight_out, gain, weight_in, weight_in, weight_out,
        ),
        check_vma=False,
    )
```

```python
import functools
import math

import jax
import jax.numpy as jnp
import numpy as np
from jax import lax
from jax.experimental import pallas as pl
from jax.experimental.pallas import tpu as pltpu
from jax.sharding import PartitionSpec as P

MESH = pl.DeviceIdType.MESH
BF16 = jnp.bfloat16
F32 = jnp.float32
TYPES = 6
LANE_DIMS = ("xa", "xb", "za", "zb")
ALL_DIMS = ("xa", "xb", "ya", "yb", "za", "zb")


class Place:
    def __init__(self):
        dp = lax.axis_index("dp")
        self.row = lax.axis_index("row")
        self.col = lax.axis_index("col")
        self.x = dp % 4
        self.yh = (dp // 4) % 2
        self.z = dp // 8
        y = self.yh * 2 + self.col
        self.bit = {
            "xa": ((self.x + 1) // 2) % 2,
            "xb": self.x // 2,
            "ya": ((y + 1) // 2) % 2,
            "yb": y // 2,
            "za": ((self.z + 1) // 2) % 2,
            "zb": self.z // 2,
        }

    def partner(self, dim):
        x, yh, z, row, col = self.x, self.yh, self.z, self.row, self.col
        if dim == "xa":
            x = x + 1 - 2 * (x % 2)
        elif dim == "xb":
            x = 3 - x
        elif dim == "za":
            z = z + 1 - 2 * (z % 2)
        elif dim == "zb":
            z = 3 - z
        elif dim in ("ya", "col"):
            col = 1 - col
        elif dim == "yb":
            col = 1 - col
            yh = 1 - yh
        elif dim == "y2":
            yh = 1 - yh
        elif dim == "row":
            row = 1 - row
        return ((z * 2 + yh) * 4 + x, row, col)


def greet(place, dims):
    barrier = pltpu.get_barrier_semaphore()
    for dim in dims:
        pl.semaphore_signal(barrier, inc=1, device_id=place.partner(dim), device_id_type=MESH)
    pl.semaphore_wait(barrier, len(dims))


def remote(place, dim, src, dst, send_sem, recv_sem):
    return pltpu.make_async_remote_copy(
        src_ref=src,
        dst_ref=dst,
        send_sem=send_sem,
        recv_sem=recv_sem,
        device_id=place.partner(dim),
        device_id_type=MESH,
    )


def exchange(value, dim, ident):
    def kernel(src, dst, send_sem, recv_sem):
        place = Place()
        greet(place, (dim,))
        copy = remote(place, dim, src, dst, send_sem, recv_sem)
        copy.start()
        copy.wait()

    return pl.pallas_call(
        kernel,
        out_shape=jax.ShapeDtypeStruct(value.shape, value.dtype),
        in_specs=[pl.BlockSpec(memory_space=pl.ANY)],
        out_specs=pl.BlockSpec(memory_space=pl.ANY),
        scratch_shapes=[pltpu.SemaphoreType.DMA, pltpu.SemaphoreType.DMA],
        compiler_params=pltpu.CompilerParams(collective_id=ident, has_side_effects=True),
        name="exchange_" + dim,
    )(value)


def span(kind, width, fixed):
    if kind == "tall":
        start, size = 0, width
        for bit in fixed:
            size //= 2
            start = start + bit * size
        return pl.ds(pl.multiple_of(start, 16) if fixed else 0, size), pl.ds(0, 128)
    rows, cols, row_start, col_start = 128, width, 0, 0
    for index, bit in enumerate(fixed):
        if index < 3:
            rows //= 2
            row_start = row_start + bit * rows
        else:
            cols //= 2
            col_start = col_start + bit * cols
    if len(fixed) > 0:
        row_start = pl.multiple_of(row_start, 16)
    if len(fixed) > 3:
        col_start = pl.multiple_of(col_start, 128)
    return pl.ds(row_start, rows), pl.ds(col_start, cols)


GATHER_ORDERS = (
    ("xa", "xb", "za", "zb"),
    ("xb", "xa", "zb", "za"),
    ("za", "zb", "xa", "xb"),
    ("zb", "za", "xb", "xa"),
)


class WeightGather:
    def __init__(self, place, index, kind, width, source, target, send_sem, recv_sem):
        self.place, self.kind, self.width = place, kind, width
        self.orders = GATHER_ORDERS + (GATHER_ORDERS[index],)
        self.whole_dim = "ya" if index == 3 else "yb"
        self.source, self.target = source, target
        self.send_sem, self.recv_sem = send_sem, recv_sem

    def part(self, ref, chunk, fixed):
        rows, cols = span(self.kind, self.width, fixed)
        if self.kind == "tall":
            return ref.at[rows, pl.ds(chunk * 128, 128)]
        return ref.at[pl.ds(pl.multiple_of(chunk * 128 + rows.start, 16), rows.size), cols]

    def copy(self, chunk, step):
        place = self.place
        sems = (self.send_sem.at[chunk, step], self.recv_sem.at[chunk, step])
        if chunk == 5:
            return remote(place, self.whole_dim, self.part(self.source, chunk, ()), self.part(self.target, chunk, ()), *sems)
        order = self.orders[chunk]
        bits = [place.bit[dim] for dim in reversed(order)]
        if step == 0:
            return remote(place, "yb", self.part(self.source, chunk, bits), self.part(self.target, chunk, bits), *sems)
        bits = bits[: 5 - step]
        part = self.part(self.target, chunk, bits)
        return remote(place, order[step - 1], part, part, *sems)

    def begin(self, chunks):
        for chunk in chunks:
            self.copy(chunk, 0).start()

    def advance(self, step):
        for chunk in range(5):
            self.copy(chunk, step - 1).wait_recv()
            self.copy(chunk, step).start()

    def finish(self):
        for chunk in range(TYPES):
            self.copy(chunk, 4 if chunk < 5 else 0).wait_recv()

    def drain(self):
        for chunk in range(TYPES):
            for step in range(5 if chunk < 5 else 1):
                self.copy(chunk, step).wait_send()


SUM_ORDERS = (
    ("xa", "xb", "ya", "yb", "za", "zb"),
    ("xb", "xa", "yb", "ya", "zb", "za"),
    ("ya", "yb", "za", "zb", "xa", "xb"),
    ("yb", "ya", "zb", "za", "xb", "xa"),
    ("za", "zb", "xa", "xb", "ya", "yb"),
    ("zb", "za", "xb", "xa", "yb", "ya"),
)
SUM_ORDERS_X = SUM_ORDERS[:2] + (("xa", "xb", "za", "zb", "ya", "yb"),) + SUM_ORDERS[3:]
SUM_ORDERS_Z = SUM_ORDERS[:2] + (("zb", "za", "xb", "xa", "ya", "yb"),) + SUM_ORDERS[3:]
ALL_HALVES = pl.ds(0, 2)


class GradSum:
    def __init__(self, place, orders, width, held, landing, stage, out, sems):
        self.place, self.kind, self.width = place, "wide", width
        self.orders = orders
        self.held, self.landing, self.stage, self.out = held, landing, stage, out
        self.send_sem, self.recv_sem, self.ag_send, self.ag_recv, self.own_sem, self.stage_sem = sems

    def view(self, ref, half, chunk, fixed):
        rows, cols = span(self.kind, self.width, fixed)
        return ref.at[half, chunk, rows, cols]

    def moves(self, chunk, step):
        place = self.place
        order = self.orders[chunk]
        dim = order[step]
        regular = [d for d in order if d != "ya"]
        p, q, c = place.bit["ya"], place.bit["yb"], place.col
        y_at = [i for i, d in enumerate(order) if d[0] == "y"]
        a_first = order[y_at[0]] == "ya"
        own = [place.bit[d] for d in order[:step] if d != "ya"]
        flipped = [1 - bit for bit in own]
        if dim[0] != "y":
            bit = place.bit[dim]
            if step < y_at[0]:
                half_own = half_land = ALL_HALVES
            else:
                half_own = c
                half_land = c if a_first else 1 - c
            sent = [(half_own, own + [1 - bit])]
            lands = [(half_land, flipped + [1 - bit])]
            kept = [(half_own, own + [bit])]
            landed = [(half_land, flipped + [bit])]
            return dim, sent, lands, kept, landed
        if a_first and dim == "ya":
            sent = [(1 - p, own + [0]), (p, own + [1])]
            lands = [(1 - p, flipped + [0]), (p, flipped + [1])]
            kept = [(p, own + [0]), (1 - p, own + [1])]
            landed = [(p, flipped + [0]), (1 - p, flipped + [1])]
        elif a_first:
            send_half = (p + 1 - q) % 2
            sent = [(send_half, own + [1 - q])]
            lands = [(c, flipped + [1 - q])]
            kept = [(c, own + [q])]
            landed = [(1 - c, flipped + [q])]
        elif dim == "yb":
            sent = [(ALL_HALVES, own + [1 - q])]
            lands = [(ALL_HALVES, flipped + [1 - q])]
            kept = [(ALL_HALVES, own + [q])]
            landed = [(ALL_HALVES, flipped + [q])]
        else:
            sent = [(1 - c, own)]
            lands = [(1 - c, flipped)]
            kept = [(c, own)]
            landed = [(c, flipped)]
        return dim, sent, lands, kept, landed

    def sends(self, chunk, step):
        dim, sent, lands, _, _ = self.moves(chunk, step)
        return [
            remote(
                self.place,
                dim,
                self.view(self.held, *region),
                self.view(self.landing, *there),
                self.send_sem.at[chunk, step, index],
                self.recv_sem.at[chunk, step, index],
            )
            for index, (region, there) in enumerate(zip(
                [(h, chunk, b) for h, b in sent], [(h, chunk, b) for h, b in lands]
            ))
        ]

    def start(self, step):
        for chunk in range(TYPES):
            for copy in self.sends(chunk, step):
                copy.start()

    def staged(self, chunk, step, slot):
        _, _, _, kept, landed = self.moves(chunk, step)
        out = []
        for index, ((half, bits), (from_half, from_bits)) in enumerate(zip(kept, landed)):
            rows, cols = span(self.kind, self.width, bits)
            both = half is ALL_HALVES
            first = 32 * slot
            if not both and len(kept) == 1 and step > 0:
                index, first = slot, 0
            target = self.stage.at[
                chunk, pl.ds(0, 2) if both else index, pl.ds(first, rows.size), pl.ds(0, cols.size)
            ]
            source = self.view(self.landing, from_half, chunk, from_bits)
            copy = pltpu.make_async_copy(source, target, self.stage_sem.at[slot, chunk, len(out)])
            out.append((copy, half, rows, cols, index, first))
        return out

    def fetch(self, step, slot):
        for chunk in range(TYPES):
            for copy in self.sends(chunk, step):
                copy.wait_recv()
            for staged in self.staged(chunk, step, slot):
                staged[0].start()

    def add(self, step, slot):
        for chunk in range(TYPES):
            for copy, half, rows, cols, index, first in self.staged(chunk, step, slot):
                copy.wait()
                for h in range(2 if half is ALL_HALVES else 1):
                    here = h if half is ALL_HALVES else half
                    there = h if half is ALL_HALVES else index

                    def body(i, carry, here=here, there=there, rows=rows, cols=cols, first=first, chunk=chunk):
                        at = pl.multiple_of(i * 16, 16)
                        mine = (here, chunk, pl.ds(pl.multiple_of(rows.start + at, 16), 16), cols)
                        came = (chunk, there, pl.ds(pl.multiple_of(first + at, 16), 16), pl.ds(0, cols.size))
                        self.held[mine] = self.held[mine] + self.stage[came]
                        return carry

                    lax.fori_loop(0, rows.size // 16, body, 0)
            if step < 5:
                for copy in self.sends(chunk, step + 1):
                    copy.start()


    def spread(self, chunk, step):
        place = self.place
        order = self.orders[chunk]
        stages = []
        for d in reversed(order):
            if d[0] == "y":
                if "y2" not in stages:
                    stages.append("y2")
            else:
                stages.append(d)
        dim = stages[step]
        keep = [d for d in order if d != "ya"]
        done = set(stages[:step])
        bits = [place.bit[d] for d in keep if ("y2" if d == "yb" else d) not in done]
        rows, cols = span(self.kind, self.width, bits)
        target = self.out.at[chunk, rows, cols]
        source = self.held.at[place.col, chunk, rows, cols] if step == 0 else target
        return remote(place, dim, source, target, self.ag_send.at[chunk, step], self.ag_recv.at[chunk, step])

    def own(self, chunk):
        place = self.place
        bits = [place.bit[d] for d in self.orders[chunk] if d != "ya"]
        rows, cols = span(self.kind, self.width, bits)
        return pltpu.make_async_copy(
            self.held.at[place.col, chunk, rows, cols], self.out.at[chunk, rows, cols], self.own_sem.at[chunk]
        )

    def spread_start(self):
        for chunk in range(TYPES):
            self.spread(chunk, 0).start()
            self.own(chunk).start()

    def spread_next(self, step):
        for chunk in range(TYPES):
            if step == 1:
                self.own(chunk).wait()
            self.spread(chunk, step - 1).wait_recv()
            self.spread(chunk, step).start()

    def finish(self):
        for chunk in range(TYPES):
            self.spread(chunk, 4).wait_recv()

    def release(self):
        for chunk in range(TYPES):
            for step in range(6):
                for copy in self.sends(chunk, step):
                    copy.wait_send()
            self.spread(chunk, 0).wait_send()

    def drain(self):
        for chunk in range(TYPES):
            for step in range(1, 5):
                self.spread(chunk, step).wait_send()


HEAD_DIM = 96
EPS = 1e-05
ROPE_BASE = 100000.0
NEG = -1e30
SCALE = 1.0 / math.sqrt(HEAD_DIM)
ANYWHERE = pl.BlockSpec(memory_space=pl.ANY)


def matmul(left, right):
    return jnp.dot(left, right, preferred_element_type=F32)


def inner_left(left, right):
    return lax.dot_general(left, right, (((0,), (0,)), ((), ())), preferred_element_type=F32)


def inner_right(left, right):
    return lax.dot_general(left, right, (((1,), (1,)), ((), ())), preferred_element_type=F32)


def rotary_tables():
    rates = ROPE_BASE ** (-2.0 * np.arange(HEAD_DIM // 2) / HEAD_DIM)
    angle = np.arange(1024)[:, None] * rates[None, :]
    cosine, sine = np.cos(angle), np.sin(angle)
    return (
        np.concatenate([cosine, cosine], axis=1).astype(np.float32),
        np.concatenate([-sine, sine], axis=1).astype(np.float32),
    )


def swap_halves(value):
    half = HEAD_DIM // 2
    return jnp.concatenate([value[:, half:], value[:, :half]], axis=1)


def head_of(value, head):
    return value[:, head * HEAD_DIM : (head + 1) * HEAD_DIM]


def pad_head(value):
    return jnp.concatenate([value, jnp.zeros((value.shape[0], 128 - HEAD_DIM), value.dtype)], axis=1)


def aligned(start, size, step):
    return pl.ds(pl.multiple_of(start, step), size)


def masked_scores(query, keys, start):
    raw = inner_right(query, keys) * SCALE
    place = start + lax.broadcasted_iota(jnp.int32, raw.shape, 0)
    return jnp.where(lax.broadcasted_iota(jnp.int32, raw.shape, 1) <= place, raw, NEG)


FORWARD_KEEPS = (
    ("gains", (8, 1536), F32),
    ("x", (512, 1536), BF16),
    ("s1", (1024, 1536), BF16),
    ("og", (512, 1536), BF16),
    ("qh", (8, 512, 128), BF16),
    ("kh", (4, 1024, 128), BF16),
    ("vh", (4, 1024, 128), BF16),
    ("attended", (512, 768), BF16),
    ("middle", (256, 1536), F32),
    ("s2", (512, 1536), BF16),
    ("hidden", (512, 2048), BF16),
    ("slope", (512, 2048), BF16),
    ("active", (512, 2048), BF16),
    ("block", (256, 1536), BF16),
)
WEIGHTS = (("wide", 2304), ("wide", 2048), ("wide", 2048), ("tall", 2048))


def weight_shape(kind, width):
    return (width, 768) if kind == "tall" else (768, width)


def forward(w_parts, w_gate, w_up, w_down, hidden_in, out_grad, gains, cosine, sine, ident):
    keeps = len(FORWARD_KEEPS)

    def kernel(*refs):
        att_parts, sources, (hid, ogr, gain, cos_t, sin_t) = refs[:4], refs[4:7], refs[7:12]
        others, kept_out = refs[12:16], refs[16 : 16 + keeps]
        refs = refs[16 + keeps :]
        v = {name: ref for (name, _, _), ref in zip(FORWARD_KEEPS, refs[:keeps])}
        (att_v, gate_v, up_v, down_v, cos_v, sin_v, oh, outgo, came1, came2, send_sem, recv_sem, small_send,
         small_recv, local_sem, load_sem, keep_sem) = refs[keeps:]
        place = Place()
        row, col = place.row, place.col
        own_cols = aligned(col * 768, 768, 128)
        their_cols = aligned((1 - col) * 768, 768, 128)
        own_rows = aligned(row * 256, 256, 256)
        their_rows = aligned((1 - row) * 256, 256, 256)
        mine = aligned(col * 256, 256, 256)
        theirs = aligned((1 - col) * 256, 256, 256)

        def small(index, dim, src, dst):
            return remote(place, dim, src, dst, small_send.at[index], small_recv.at[index])

        def local(index, src, dst):
            return pltpu.make_async_copy(src, dst, local_sem.at[index])

        keep_order = [name for name, _, _ in FORWARD_KEEPS]

        def keep(name):
            index = keep_order.index(name)
            return pltpu.make_async_copy(v[name], kept_out[index], keep_sem.at[index])

        att_loads = [
            local(5 + k, part, att_v.at[own_cols, pl.ds(at, part.shape[1])])
            for k, (part, at) in enumerate(zip(att_parts, (0, 768, 1152, 1536)))
        ]
        x_load = local(0, hid, v["x"].at[:, own_cols])
        gain_load = local(1, gain, v["gains"].at[:, own_cols])
        og_load = local(2, ogr.at[mine], v["og"].at[own_rows, own_cols])
        cos_load = local(3, cos_t, cos_v)
        sin_load = local(4, sin_t, sin_v)
        for copy in att_loads + [x_load, gain_load, og_load, cos_load, sin_load]:
            copy.start()
        greet(place, ALL_DIMS + ("row",))
        x_moves = [
            small(k, "ya", hid.at[pl.ds(k * 256, 256)], v["x"].at[pl.ds(k * 256, 256), own_cols]) for k in range(2)
        ]
        gain_move = small(2, "ya", gain, v["gains"].at[:, own_cols])
        og_move = small(3, "ya", ogr.at[theirs], v["og"].at[own_rows, own_cols])
        gain_move.start()
        for copy in x_moves:
            copy.start()
        jobs = [
            WeightGather(place, index, kind, width, source, other, send_sem.at[index], recv_sem.at[index])
            for index, ((kind, width), source, other) in enumerate(
                zip(WEIGHTS, (att_v.at[own_cols],) + tuple(sources), others)
            )
        ]
        att, gate_j, up_j, down_j = jobs
        mlp = (gate_j, up_j, down_j)
        for copy in att_loads:
            copy.wait()
        att.begin(range(5))
        for job in mlp:
            job.begin(range(5))
        att.begin((5,))
        whole = (att_v, gate_v, up_v, down_v)
        own_loads, other_loads = [None], []
        for index, ((kind, _), other, target) in enumerate(zip(WEIGHTS, others, whole)):
            tall = kind == "tall"
            if index > 0:
                own_loads.append(
                    pltpu.make_async_copy(
                        sources[index - 1], target.at[:, own_cols] if tall else target.at[own_cols], load_sem.at[0, index]
                    )
                )
                own_loads[index].start()
            other_loads.append(
                pltpu.make_async_copy(
                    other, target.at[:, their_cols] if tall else target.at[their_cols], load_sem.at[1, index]
                )
            )

        def norm_into(read, gain_row, target, start):
            def block(i, carry):
                value = read(i)
                factor = lax.rsqrt(jnp.mean(value * value, axis=1, keepdims=True) + EPS)
                target[aligned(start + i * 32, 32, 32)] = (
                    value * factor * v["gains"][gain_row : gain_row + 1, :]
                ).astype(BF16)
                return carry

            lax.fori_loop(0, 8, block, 0)

        x_load.wait()
        gain_load.wait()
        gain_move.wait_recv()
        att.advance(1)
        s1_moves = []
        for part in range(2):
            x_moves[part].wait_recv()
            start = row * 512 + part * 256
            norm_into(lambda i: v["x"][aligned(part * 256 + i * 32, 32, 32)].astype(F32), 0, v["s1"], start)
            rows = aligned(start, 256, 256)
            s1_moves.append(small(4 + part, "row", v["s1"].at[rows], v["s1"].at[rows]))
            s1_moves[part].start()
            if part == 0:
                att.advance(2)
                for job in mlp:
                    job.advance(1)
                att.advance(3)
        og_move.start()
        att.advance(4)
        for job in mlp:
            job.advance(2)
        for job in mlp:
            job.begin((5,))
        keep("x").start()
        keep("gains").start()
        cos_load.wait()
        sin_load.wait()
        for copy in s1_moves:
            copy.wait_recv()
        keep("s1").start()
        att.finish()
        other_loads[0].start()
        for job in mlp:
            job.advance(3)
        other_loads[0].wait()

        def turned(value, rows):
            return value * cos_v[rows] + swap_halves(value) * sin_v[rows]

        for part in range(4):
            rows = slice(part * 256, part * 256 + 256)
            value = matmul(v["s1"][rows], att_v[:, 768:1536])
            for head in range(4):
                v["kh"][head, rows] = pad_head(turned(head_of(value, head), rows).astype(BF16))
                v["vh"][head, rows] = pad_head(head_of(value, 4 + head).astype(BF16))
        for part in range(2):
            places = aligned(part * 512 + col * 256, 256, 256)
            rows = slice(part * 256, part * 256 + 256)
            value = matmul(v["s1"][places], att_v[:, 0:768])
            for head in range(8):
                v["qh"][head, rows] = pad_head(turned(head_of(value, head), places).astype(BF16))
        for name in ("qh", "kh", "vh"):
            keep(name).start()

        def heads(h, carry):
            for pair in range(2):
                for at, reach in ((0, 512), (256, 1024)):
                    scores = masked_scores(
                        v["qh"][h * 2 + pair, at : at + 256], v["kh"][h, 0:reach], at * 2 + col * 256
                    )
                    powers = jnp.exp(scores - jnp.max(scores, axis=1, keepdims=True))
                    total = jnp.sum(powers, axis=1, keepdims=True)
                    shares = (powers * (1.0 / total)).astype(BF16)
                    oh[h * 2 + pair, at : at + 256] = matmul(shares, v["vh"][h, 0:reach]).astype(BF16)
            return carry

        lax.fori_loop(0, 2, heads, 0)
        for job in mlp:
            job.advance(4)
        lax.fori_loop(2, 4, heads, 0)
        v["attended"][...] = jnp.concatenate([oh[j][:, 0:HEAD_DIM] for j in range(8)], axis=1)
        keep("attended").start()

        def summed(index, read, weight, came, done):
            def half(rows, put):
                left = read(rows)
                for h in range(3):
                    put(h, matmul(left, weight(h)))

            def put_out(h, value):
                outgo[:, h * 512 : h * 512 + 512] = value

            half(their_rows, put_out)
            move = small(index, "row", outgo, came)
            move.start()
            half(own_rows, done)
            move.wait_recv()
            return move

        def out_weight(h):
            if h == 0:
                return att_v[0:768, 1536 : 1536 + 512]
            if h == 2:
                return att_v[768:1536, 1536 + 256 : 2304]
            return jnp.concatenate([att_v[0:768, 2048:2304], att_v[768:1536, 1536:1792]], axis=1)

        def add_middle(h, value):
            at = h * 512
            v["middle"][:, at : at + 512] = v["x"][mine, at : at + 512].astype(F32) + value

        out_move = summed(6, lambda rows: v["attended"][rows], out_weight, came1, add_middle)
        v["middle"][...] = v["middle"][...] + came1[...]
        keep("middle").start()
        norm_into(lambda i: v["middle"][aligned(i * 32, 32, 32)], 1, v["s2"], row * 256)
        s2_move = small(7, "row", v["s2"].at[own_rows], v["s2"].at[own_rows])
        s2_move.start()
        og_load.wait()
        og_move.wait_recv()
        og_swap = small(8, "row", v["og"].at[own_rows], v["og"].at[own_rows])
        og_swap.start()
        for index, job in ((1, gate_j), (2, up_j)):
            own_loads[index].wait()
            job.finish()
            other_loads[index].start()
        s2_move.wait_recv()
        keep("s2").start()
        og_swap.wait_recv()
        keep("og").start()
        other_loads[1].wait()
        other_loads[2].wait()

        def units(n, carry):
            cols = aligned(n * 256, 256, 256)
            gate = matmul(v["s2"][...], gate_v[:, cols])
            upper = matmul(v["s2"][...], up_v[:, cols])
            logistic = 1.0 / (1.0 + jnp.exp(-gate))
            active = gate * logistic
            v["hidden"][:, cols] = (active * upper).astype(BF16)
            v["slope"][:, cols] = (upper * logistic * (1.0 + gate * (1.0 - logistic))).astype(BF16)
            v["active"][:, cols] = active.astype(BF16)
            return carry

        lax.fori_loop(0, 8, units, 0)
        for name in ("hidden", "slope", "active"):
            keep(name).start()
        own_loads[3].wait()
        down_j.finish()
        other_loads[3].start()
        out_move.wait_send()
        other_loads[3].wait()

        def add_out(h, value):
            at = h * 512
            came1[:, at : at + 512] = v["middle"][:, at : at + 512] + value

        down_move = summed(
            9, lambda rows: v["hidden"][rows], lambda h: down_v[:, h * 512 : h * 512 + 512], came2, add_out
        )
        v["block"][...] = (came1[...] + came2[...]).astype(BF16)
        keep("block").start()
        for job in jobs:
            job.drain()
        for copy in x_moves + s1_moves + [gain_move, og_move, s2_move, og_swap, down_move]:
            copy.wait_send()
        for name in keep_order:
            keep(name).wait()

    outs = [jax.ShapeDtypeStruct(weight_shape(*w), BF16) for w in WEIGHTS]
    outs += [jax.ShapeDtypeStruct(shape, kind) for _, shape, kind in FORWARD_KEEPS]
    return pl.pallas_call(
        kernel,
        out_shape=outs,
        in_specs=[ANYWHERE] * 12,
        out_specs=[ANYWHERE] * (4 + keeps),
        scratch_shapes=[pltpu.VMEM(shape, kind) for _, shape, kind in FORWARD_KEEPS]
        + [
            pltpu.VMEM((1536, 2304), BF16),
            pltpu.VMEM((1536, 2048), BF16),
            pltpu.VMEM((1536, 2048), BF16),
            pltpu.VMEM((2048, 1536), BF16),
            pltpu.VMEM((1024, HEAD_DIM), F32),
            pltpu.VMEM((1024, HEAD_DIM), F32),
            pltpu.VMEM((8, 512, 128), BF16),
            pltpu.VMEM((256, 1536), F32),
            pltpu.VMEM((256, 1536), F32),
            pltpu.VMEM((256, 1536), F32),
            pltpu.SemaphoreType.DMA((4, TYPES, 5)),
            pltpu.SemaphoreType.DMA((4, TYPES, 5)),
            pltpu.SemaphoreType.DMA((10,)),
            pltpu.SemaphoreType.DMA((10,)),
            pltpu.SemaphoreType.DMA((9,)),
            pltpu.SemaphoreType.DMA((2, 4)),
            pltpu.SemaphoreType.DMA((keeps,)),
        ],
        compiler_params=pltpu.CompilerParams(
            collective_id=ident, has_side_effects=True, vmem_limit_bytes=63 << 20
        ),
        name="forward",
    )(*w_parts, w_gate, w_up, w_down, hidden_in, out_grad, gains, cosine, sine)


GROUP_WIDTHS = (2048, 2048, 2048, 2560)
SERVED = {
    "gated": "",
    "up": "",
    "e0": "D",
    "e1": "d",
    "e2": "",
    "e3": "",
    "e4": "",
    "expanded": "G",
    "normed": "g",
    "attended": "D",
    "head0": "dU",
    "head1": "uG",
    "head2": "gD",
    "heads": "dU",
    "packed": "uG",
    "projected": "",
    "started": "gDdUuAaGgDdUu",
    "input": "AaGg",
    "done": "UuAaDdGgUu",
    "rest": "nAanAanAanmndguandguandguadguadgua",
}


def backward(w_parts, mlp_weights, other_weights, kept, cosine, sine, ident):
    keeps = len(FORWARD_KEEPS)
    groups = len(GROUP_WIDTHS)
    names = [name for name, _, _ in FORWARD_KEEPS]

    def kernel(*refs):
        att_parts, (w_gate, w_up, w_down), (o_att, o_gate, o_up, o_down) = refs[0:4], refs[4:7], refs[7:11]
        hbm = dict(zip(names, refs[11 : 11 + keeps]))
        cos_t, sin_t = refs[11 + keeps : 13 + keeps]
        refs = refs[13 + keeps :]
        sums, landing, (bo_out, ig_out, gain_out) = refs[:groups], refs[groups : 2 * groups], refs[2 * groups : 2 * groups + 3]
        (held0, held1, held2, acts, stage, pool, og, qh, kh, vh, doh, attended, dk, dv, part_kv, kv_in,
         dqkv, cos_v, sin_v, outgo, mine_v, came1, came2, middle, x_v, gains, gain_sum, gain_came, ig_v, bo_v,
         rs_send, rs_recv, ag_send, ag_recv, own_sem, stage_sem, load_sem, pool_sem, small_send, small_recv,
        ) = refs[2 * groups + 3 :]
        place = Place()
        row, col = place.row, place.col
        own_cols = aligned(col * 768, 768, 128)
        their_cols = aligned((1 - col) * 768, 768, 128)
        own_rows = aligned(row * 256, 256, 256)
        their_rows = aligned((1 - row) * 256, 256, 256)
        mine = aligned(col * 256, 256, 256)
        theirs = aligned((1 - col) * 256, 256, 256)

        def small(index, dim, src, dst):
            return remote(place, dim, src, dst, small_send.at[index], small_recv.at[index])

        held = (held0, held1, held2, acts)
        flat = acts.reshape(2 * TYPES * 128, 2560)
        slope, active, units = (flat.at[pl.ds(k * 512, 512), pl.ds(0, 2048)] for k in range(3))
        orders = (SUM_ORDERS,) * 4
        down, gate, up, att = [
            GradSum(
                place, orders[g], width, held[g], landing[g], stage, sums[g],
                (rs_send.at[g], rs_recv.at[g], ag_send.at[g], ag_recv.at[g], own_sem.at[g], stage_sem),
            )
            for g, width in enumerate(GROUP_WIDTHS)
        ]
        served, fetched = {}, {}

        def serve(point):
            for letter in SERVED[point]:
                name = letter.lower()
                step = served.get(name, 0)
                job = {"d": down, "g": gate, "u": up, "a": att}.get(name)
                if job is not None and step < 6 and name not in fetched:
                    free = {0, 1} - set(fetched.values())
                    assert 0 in free if step == 0 else free
                    assert step > 0 or len(free) == 2
                    fetched[name] = min(free)
                    job.fetch(step, fetched[name])
                if letter != name:
                    continue
                if name == "m":
                    bo_move.start()
                    ig_move.start()
                    continue
                served[name] = step + 1
                if job is None:
                    gain_step(step + 1)
                elif step < 6:
                    job.add(step, fetched.pop(name))
                    if step == 5:
                        job.spread_start()
                elif step < 10:
                    job.spread_next(step - 5)
                else:
                    job.finish()

        loads = {}

        def load(name, source, target):
            copy = pltpu.make_async_copy(source, target, load_sem.at[len(loads)])
            copy.start()
            loads[name] = copy

        def down_tile(n):
            at = pl.ds(pl.multiple_of(1024 + (n % 2) * 256, 256), 256)
            rows = pl.ds(pl.multiple_of(n * 256, 256), 256)
            return [
                pltpu.make_async_copy(w_down.at[rows], pool.at[at, own_cols], pool_sem.at[n % 2, 0]),
                pltpu.make_async_copy(o_down.at[rows], pool.at[at, their_cols], pool_sem.at[n % 2, 1]),
            ]

        def expand_tile(n):
            sources = (w_gate, w_up) if n < 3 else (o_gate, o_up)
            rows = pl.ds((n % 3) * 256, 256)
            slot = n % 2
            return [
                pltpu.make_async_copy(
                    source.at[rows], pool.at[pl.ds((slot * 2 + k) * 256, 256)], pool_sem.at[2 + slot, k]
                )
                for k, source in enumerate(sources)
            ]

        load("og", hbm["og"], og)
        load("hidden", hbm["hidden"], units)
        for copy in down_tile(0):
            copy.start()
        load("slope", hbm["slope"], slope)
        load("active", hbm["active"], active)
        for n in range(2):
            for copy in expand_tile(n):
                copy.start()
        load("middle", hbm["middle"], middle)
        load("gains", hbm["gains"], gains)
        load("qh", hbm["qh"], qh)
        load("kh", hbm["kh"], kh)
        load("vh", hbm["vh"], vh)
        load("attended", hbm["attended"], attended)
        load("cos", cos_t, cos_v)
        load("sin", sin_t, sin_v)
        load("x", hbm["x"].at[mine], x_v)
        load("block", hbm["block"], bo_v)
        greet(place, ALL_DIMS + ("y2", "row"))

        def weight_grad(left, right, target, at, blocks, cols):
            def block(i, carry):
                half, pair = i // 3, i % 3
                lhs = left[:, aligned(i * 256, 256, 256)]
                for n in range(cols // 512):
                    value = inner_left(lhs, right[:, n * 512 : n * 512 + 512]).astype(BF16)
                    for k in range(2):
                        target[half, pair * 2 + k, :, at + n * 512 : at + n * 512 + 512] = value[k * 128 : k * 128 + 128]
                return carry

            lax.fori_loop(0, blocks, block, 0)

        loads["og"].wait()
        loads["hidden"].wait()
        weight_grad(og, units, held0, 0, 6, 2048)
        down.start(0)
        load("s2", hbm["s2"], units.at[:, pl.ds(0, 1536)])
        loads["slope"].wait()
        loads["active"].wait()

        def hidden_tile(n, carry):
            @pl.when(n < 7)
            def _():
                for copy in down_tile(n + 1):
                    copy.start()

            for copy in down_tile(n):
                copy.wait()
            weight = pool[pl.ds(pl.multiple_of(1024 + (n % 2) * 256, 256), 256), 0:1536]
            grad = inner_right(og[...], weight)
            cols = aligned(n * 256, 256, 256)
            slope[:, cols] = (grad * slope[:, cols].astype(F32)).astype(BF16)
            active[:, cols] = (grad * active[:, cols].astype(F32)).astype(BF16)
            return carry

        lax.fori_loop(0, 8, hidden_tile, 0)
        loads["s2"].wait()
        weight_grad(units, slope, held1, 0, 6, 2048)
        gate.start(0)
        serve("gated")
        weight_grad(units, active, held2, 0, 6, 2048)
        up.start(0)
        serve("up")
        loads["block"].wait()
        bo_move = small(6, "ya", bo_v.at[:, their_cols], bo_out.at[mine])
        bo_own = pltpu.make_async_copy(bo_v.at[:, own_cols], bo_out.at[mine], pool_sem.at[4, 0])
        bo_own.start()

        for n in range(6):
            for copy in expand_tile(n):
                copy.wait()
            slot = (n % 2) * 512
            cols = aligned((col if n < 3 else 1 - col) * 768 + (n % 3) * 256, 256, 256)
            for rows, target in ((their_rows, outgo), (own_rows, mine_v)):
                target[:, cols] = inner_right(slope[rows], pool[slot : slot + 256, :]) + inner_right(
                    active[rows], pool[slot + 256 : slot + 512, :]
                )
            if n + 2 < 6:
                for copy in expand_tile(n + 2):
                    copy.start()
            if n < 5:
                serve("e%d" % n)
        mlp_move = small(0, "row", outgo, came1)
        mlp_move.start()
        load("out_own", att_parts[3], pool.at[pl.ds(0, 768), own_cols])
        load("out_other", o_att.at[:, pl.ds(1536, 768)], pool.at[pl.ds(0, 768), their_cols])
        serve("expanded")
        loads["middle"].wait()
        loads["gains"].wait()
        mlp_move.wait_recv()

        gain_sum[0] = jnp.zeros((8, 1536), F32)

        def norm_back(value_of, grad_came, gain_row, finish):

            def block(i, carry):
                rows = aligned(i * 32, 32, 32)
                value = value_of(rows)
                grad = mine_v[rows] + grad_came[rows]
                factor = lax.rsqrt(jnp.mean(value * value, axis=1, keepdims=True) + EPS)
                normed = value * factor
                gain_sum[0, gain_row : gain_row + 1, :] += jnp.sum(grad * normed, axis=0, keepdims=True)
                scaled = grad * gains[gain_row : gain_row + 1, :]
                back = factor * (scaled - normed * jnp.mean(scaled * normed, axis=1, keepdims=True))
                finish(i, rows, back)
                return carry

            lax.fori_loop(0, 8, block, 0)

        def put_middle(i, rows, back):
            at = aligned(row * 256 + i * 32, 32, 32)
            total = og[at].astype(F32) + back
            middle[rows] = total
            og[at] = total.astype(BF16)

        norm_back(lambda rows: middle[rows], came1, 1, put_middle)
        gm_move = small(1, "row", og.at[own_rows], og.at[own_rows])
        gm_move.start()
        loads["out_own"].wait()
        loads["out_other"].wait()
        serve("normed")
        gm_move.wait_recv()

        for part in range(2):
            value = inner_right(og[...], pool[part * 384 : part * 384 + 384, 0:1536]).astype(BF16)
            for head in range(4):
                doh[part * 4 + head] = pad_head(value[:, head * HEAD_DIM : (head + 1) * HEAD_DIM])
        load("s1", hbm["s1"], pool.at[pl.ds(0, 1024), pl.ds(0, 1536)])
        serve("attended")
        for name in ("qh", "kh", "vh", "cos", "sin"):
            loads[name].wait()

        def turned_back(value, places):
            return value * cos_v[places] - swap_halves(value) * sin_v[places]

        def heads(h, carry):
            dk[...] = jnp.zeros((1024, 128), F32)
            dv[...] = jnp.zeros((1024, 128), F32)
            for pair in range(2):
                for at, reach in ((0, 512), (256, 1024)):
                    rows = slice(at, at + 256)
                    query, grad = qh[h * 2 + pair, rows], doh[h * 2 + pair, rows]
                    keys, values = kh[h, 0:reach], vh[h, 0:reach]
                    scores = masked_scores(query, keys, at * 2 + col * 256)
                    powers = jnp.exp(scores - jnp.max(scores, axis=1, keepdims=True))
                    shares = powers * (1.0 / jnp.sum(powers, axis=1, keepdims=True))
                    grad_shares = inner_right(grad, values)
                    center = jnp.sum(grad_shares * shares, axis=1, keepdims=True)
                    grad_raw = (shares * (grad_shares - center) * SCALE).astype(BF16)
                    dk[0:reach] += inner_left(grad_raw, query)
                    dv[0:reach] += inner_left(shares.astype(BF16), grad)
                    value = turned_back(matmul(grad_raw, keys)[:, 0:HEAD_DIM], aligned(at * 2 + col * 256, 256, 256))
                    qh[h * 2 + pair, rows] = pad_head(value.astype(BF16))
            for part in range(4):
                rows = slice(part * 256, part * 256 + 256)
                kh[h, rows] = pad_head(turned_back(dk[rows, 0:HEAD_DIM], rows).astype(BF16))
            vh[h] = dv[...].astype(BF16)
            return carry

        for h in range(4):
            lax.fori_loop(h, h + 1, heads, 0)
            if h < 3:
                serve("head%d" % h)
        serve("heads")
        for part in range(4):
            rows = slice(part * 256, part * 256 + 256)
            part_kv[rows] = jnp.concatenate(
                [kh[h, rows][:, 0:HEAD_DIM] for h in range(4)] + [vh[h, rows][:, 0:HEAD_DIM] for h in range(4)], axis=1
            )
        kv_moves = [
            small(2 + part, "ya", part_kv.at[aligned(part * 512 + (1 - col) * 256, 256, 256)],
                  kv_in.at[pl.ds(part * 256, 256)])
            for part in range(2)
        ]
        for copy in kv_moves:
            copy.start()
        dqkv[:, 0:768] = jnp.concatenate([qh[j][:, 0:HEAD_DIM] for j in range(8)], axis=1)
        serve("packed")
        loads["s1"].wait()
        loads["attended"].wait()

        def projection_grads(i, carry):
            half, pair = i // 3, i % 3
            features = aligned(i * 256, 256, 256)
            parts = [pool[aligned(part * 512 + col * 256, 256, 256), features] for part in range(2)]
            whole = pool[0:1024, features]

            def put(at, value):
                value = value.astype(BF16)
                for k in range(2):
                    acts[half, pair * 2 + k, :, at : at + 384] = value[k * 128 : k * 128 + 128]

            for n in range(2):
                cols = slice(n * 384, n * 384 + 384)
                put(n * 384, inner_left(parts[0], dqkv[0:256, cols]) + inner_left(parts[1], dqkv[256:512, cols]))
                put(768 + n * 384, inner_left(whole, part_kv[:, cols]))
            return carry

        lax.fori_loop(0, 6, projection_grads, 0)
        serve("projected")
        load("qkv_other", o_att.at[:, pl.ds(0, 1536)], pool.at[their_cols, pl.ds(0, 1536)])
        for k, at in enumerate((0, 768, 1152)):
            load(k, att_parts[k], pool.at[own_cols, pl.ds(at, att_parts[k].shape[1])])

        def out_grads(i, carry):
            lhs = attended[:, aligned(i * 256, 256, 256)]
            for half in range(2):
                value = inner_left(lhs, og[:, half * 768 : half * 768 + 768]).astype(BF16)
                for k in range(2):
                    acts[half, i * 2 + k, :, 1536:2304] = value[k * 128 : k * 128 + 128]
            return carry

        lax.fori_loop(0, 3, out_grads, 0)
        acts[:, :, :, 2304:2560] = jnp.zeros((2, TYPES, 128, 256), BF16)
        att.start(0)

        serve("started")
        for copy in kv_moves:
            copy.wait_recv()
        for part in range(2):
            rows = slice(part * 256, part * 256 + 256)
            own = part_kv[aligned(part * 512 + col * 256, 256, 256)].astype(F32)
            dqkv[rows, 768:1536] = (own + kv_in[rows].astype(F32)).astype(BF16)
        loads["qkv_other"].wait()
        for k in range(3):
            loads[k].wait()
        mlp_move.wait_send()
        for n in range(3):
            cols = slice(n * 512, n * 512 + 512)
            for rows, target in ((their_rows, outgo), (own_rows, mine_v)):
                target[:, cols] = inner_right(dqkv[rows], pool[cols, 0:1536])
        att_move = small(4, "row", outgo, came2)
        att_move.start()
        serve("input")
        loads["x"].wait()
        att_move.wait_recv()

        def put_input(i, rows, back):
            ig_v[rows] = (middle[rows] + back).astype(BF16)

        norm_back(lambda rows: x_v[rows].astype(F32), came2, 0, put_input)
        ig_move = small(5, "ya", ig_v.at[:, their_cols], ig_out.at[mine])
        ig_own = pltpu.make_async_copy(ig_v.at[:, own_cols], ig_out.at[mine], pool_sem.at[4, 1])
        ig_own.start()

        gain_dims = ("row",) + ALL_DIMS
        gain_moves = [small(7 + k, dim, gain_sum.at[k], gain_came.at[k]) for k, dim in enumerate(gain_dims)]

        def gain_step(k):
            if k > 0:
                gain_moves[k - 1].wait_recv()
                gain_sum[k] = gain_sum[k - 1] + gain_came[k - 1]
            if k < len(gain_dims):
                gain_moves[k].start()

        gain_step(0)

        serve("done")
        serve("rest")
        gain_own = pltpu.make_async_copy(gain_sum.at[7, :, own_cols], gain_out, pool_sem.at[4, 0])
        bo_own.wait()
        gain_own.start()
        ig_own.wait()
        gain_own.wait()
        for copy in [gm_move, att_move] + kv_moves + gain_moves:
            copy.wait_send()
        ig_move.wait()
        bo_move.wait()
        for job in (down, gate, up, att):
            job.release()
        for job in (down, gate, up, att):
            job.drain()

    chunk_shapes = [(TYPES, 128, width) for width in GROUP_WIDTHS]
    outs = [jax.ShapeDtypeStruct(shape, BF16) for shape in chunk_shapes]
    outs += [jax.ShapeDtypeStruct((2,) + shape, BF16) for shape in chunk_shapes]
    outs += [jax.ShapeDtypeStruct((512, 768), BF16)] * 2 + [jax.ShapeDtypeStruct((8, 768), F32)]
    dma = pltpu.SemaphoreType.DMA
    return pl.pallas_call(
        kernel,
        out_shape=outs,
        in_specs=[ANYWHERE] * (13 + keeps),
        out_specs=[ANYWHERE] * len(outs),
        scratch_shapes=[
            pltpu.VMEM((2, TYPES, 128, 2048), BF16),
            pltpu.VMEM((2, TYPES, 128, 2048), BF16),
            pltpu.VMEM((2, TYPES, 128, 2048), BF16),
            pltpu.VMEM((2, TYPES, 128, 2560), BF16),
            pltpu.VMEM((TYPES, 2, 64, 2560), BF16),
            pltpu.VMEM((1536, 2048), BF16),
            pltpu.VMEM((512, 1536), BF16),
            pltpu.VMEM((8, 512, 128), BF16),
            pltpu.VMEM((4, 1024, 128), BF16),
            pltpu.VMEM((4, 1024, 128), BF16),
            pltpu.VMEM((8, 512, 128), BF16),
            pltpu.VMEM((512, 768), BF16),
            pltpu.VMEM((1024, 128), F32),
            pltpu.VMEM((1024, 128), F32),
            pltpu.VMEM((1024, 768), BF16),
            pltpu.VMEM((512, 768), BF16),
            pltpu.VMEM((512, 1536), BF16),
            pltpu.VMEM((1024, HEAD_DIM), F32),
            pltpu.VMEM((1024, HEAD_DIM), F32),
            pltpu.VMEM((256, 1536), F32),
            pltpu.VMEM((256, 1536), F32),
            pltpu.VMEM((256, 1536), F32),
            pltpu.VMEM((256, 1536), F32),
            pltpu.VMEM((256, 1536), F32),
            pltpu.VMEM((256, 1536), BF16),
            pltpu.VMEM((8, 1536), F32),
            pltpu.VMEM((8, 8, 1536), F32),
            pltpu.VMEM((7, 8, 1536), F32),
            pltpu.VMEM((256, 1536), BF16),
            pltpu.VMEM((256, 1536), BF16),
            dma((groups, TYPES, 6, 2)),
            dma((groups, TYPES, 6, 2)),
            dma((groups, TYPES, 5)),
            dma((groups, TYPES, 5)),
            dma((groups, TYPES)),
            dma((2, TYPES, 2)),
            dma((24,)),
            dma((5, 2)),
            dma((14,)),
            dma((14,)),
        ],
        compiler_params=pltpu.CompilerParams(
            collective_id=ident, has_side_effects=True, vmem_limit_bytes=63 << 20
        ),
        name="backward",
    )(*w_parts, *mlp_weights, *other_weights, *kept, cosine, sine)


def widen(sum_down, sum_gate, sum_up, sum_att):
    def kernel(down, gate, up, att, query_out, key_out, value_out, out_out, gate_out, up_out, down_out):
        at = 0
        for target in (query_out, key_out, value_out, out_out):
            width = target.shape[1]
            target[...] = att[0, :, at : at + width].astype(F32)
            at += width
        gate_out[...] = gate[0].astype(F32)
        up_out[...] = up[0].astype(F32)
        down_out[...] = down[0].astype(F32).T

    widths = (768, 384, 384, 768, 2048, 2048)
    return pl.pallas_call(
        kernel,
        grid=(TYPES,),
        out_shape=[jax.ShapeDtypeStruct((768, width), F32) for width in widths]
        + [jax.ShapeDtypeStruct((2048, 768), F32)],
        in_specs=[pl.BlockSpec((1, 128, width), lambda i: (i, 0, 0)) for width in GROUP_WIDTHS],
        out_specs=[pl.BlockSpec((128, width), lambda i: (i, 0)) for width in widths]
        + [pl.BlockSpec((2048, 128), lambda i: (0, i))],
        compiler_params=pltpu.CompilerParams(vmem_limit_bytes=62 << 20),
        name="widen",
    )(sum_down, sum_gate, sum_up, sum_att)


def per_device(
    hidden_in, gain_attn, w_query, w_key, w_value, w_out, gain_mlp, w_gate, w_up, w_down, out_grad
):
    w_parts = (w_query, w_key, w_value, w_out)
    gains = jnp.concatenate([gain_attn[None], gain_mlp[None], jnp.zeros((6, 768), F32)], axis=0)
    cosine, sine = (jnp.asarray(table) for table in rotary_tables())
    done = forward(w_parts, w_gate, w_up, w_down, hidden_in, out_grad, gains, cosine, sine, 1)
    back = backward(w_parts, (w_gate, w_up, w_down), done[:4], done[4:], cosine, sine, 2)
    block_out, in_grad, gain_grads = back[8:]
    sums = widen(*back[:4])
    return (block_out, in_grad, gain_grads[0]) + tuple(sums[:4]) + (gain_grads[1],) + tuple(sums[4:])


def solution(mesh):
    tokens, weight_in, weight_out, gain = P(("dp", "row"), "col"), P("col", "row"), P("row", "col"), P("col")
    return jax.shard_map(
        per_device,
        mesh=mesh,
        in_specs=(
            tokens, gain, weight_in, weight_in, weight_in, weight_out, gain, weight_in, weight_in, weight_out, tokens,
        ),
        out_specs=(
            tokens, tokens, gain, weight_in, weight_in, weight_in, weight_out, gain, weight_in, weight_in, weight_out,
        ),
        check_vma=False,
    )
```
